32 devices in a mesh: seq: 16 (over z, x, core), tp: 2 (over y).
Axes of the slice: x: 2, y: 2, z: 4, core: 2. Of those that a mesh axis runs over, the one named last changes fastest.
Arguments:
- q_feat: bfloat16 [4096, 4096], P('seq', 'tp'), may hold values from -6 to 6
- k_feat: bfloat16 [4096, 4096], P('seq', 'tp'), may hold values from -6 to 6
- v_feat: bfloat16 [4096, 4096], P('seq', 'tp'), may hold values from -6 to 6
- stream: bfloat16 [4096, 4096], P('seq', 'tp'), may hold values from -6 to 6
- filters: float32 [4096, 4096], P(('tp', 'seq')), may hold values from -1.2 to 1.2
- w_out: bfloat16 [4096, 4096], P('tp', 'seq'), may hold values from -0.125 to 0.125
Outputs:
- mixed_out: bfloat16 [4096, 4096], P('seq', 'tp')
The draws below stay inside these ranges and needn't reach their ends.
All inputs are finite; a program needn't handle non-finite values.
Results may differ from the reference program's by a relative error of at most 0.012.
Values may be sent and summed in bfloat16 or wider, within the bound.
A program may use at most 128 MiB of HBM per device.

```python
import math
import jax
import jax.numpy as jnp
from jax import lax

D = 4096
L = 4096


def draw_filters(key, part):
    keys = jax.random.split(jax.random.fold_in(key, 71), 6)
    segment_starts = jnp.arange(L, dtype=jnp.float32)
    spans = jnp.exp(jax.random.uniform(keys[0], (D,), jnp.float32, math.log(30.0), math.log(64.0 * L)))
    amplitude = jnp.sqrt(1.0 - jnp.exp(-2.0 / spans))
    noise = jax.random.truncated_normal(keys[3], -4.0, 4.0, (D, L), jnp.float32)
    sequence_indices = jax.random.randint(keys[4], (D, 4), 0, L)
    discarded_entries = jax.random.uniform(keys[5], (D, 4), jnp.float32, 0.5, 0.8)
    normalizing_multiplier = jnp.ones((D, L), jnp.float32)
    for kernel_tap_group in range(4):
        normalizing_multiplier = normalizing_multiplier * jnp.where(segment_starts[None, :] >= sequence_indices[:, kernel_tap_group:kernel_tap_group + 1].astype(jnp.float32), discarded_entries[:, kernel_tap_group:kernel_tap_group + 1], 1.0)
    base = amplitude[:, None] * jnp.exp(-segment_starts[None, :] / spans[:, None]) * normalizing_multiplier
    return base * noise


def raised(values, own_key, source, target, parts, factor):
    def block_of(position):
        return (jnp.arange(values.shape[position]) // (values.shape[position] // parts)).reshape((-1,) + (1,) * (values.ndim - 1 - position))

    near = jax.random.permutation(own_key, parts)[block_of(target)]
    other_side = (block_of(target) + parts // 2) % parts
    return jnp.where((block_of(source) == near) | (block_of(source) == other_side), factor * values, values)


def block_levels(own_key, shape, cuts, least, top_value):
    def one(dim, shards_of):
        steps = jax.random.uniform(jax.random.fold_in(jax.random.fold_in(own_key, 6), dim), (shards_of,), jnp.float32, least / len(cuts), top_value / len(cuts))
        return jnp.repeat(jnp.exp(steps), shape[dim] // shards_of).reshape((-1,) + (1,) * (len(shape) - dim - 1))

    level = one(*cuts[0])
    for cut in cuts[1:]:
        level = level * one(*cut)
    return level


def scatter_about(stream_key, extent, deviation, reach, shards=(), held_as=jnp.bfloat16):
    entries = deviation * jax.random.normal(stream_key, extent, jnp.float32)
    if shards:
        entries = entries * block_levels(stream_key, extent, shards, -0.22, 0.18)
    return jnp.clip(entries, -reach, reach).astype(held_as)


def bell_draw_with(stream_key, dims, width, most, shards, heavy, kind=jnp.bfloat16):
    array = width * jax.random.normal(stream_key, dims, jnp.float32)
    if shards:
        array = array * block_levels(stream_key, dims, shards, -0.22, 0.18)
    return jnp.clip(raised(array, jax.random.fold_in(stream_key, 3), *heavy), -most, most).astype(kind)


def setup_inputs(seed: int = 0) -> dict:
    splits = jax.random.split(jax.random.key(seed), 7)
    q_feat = scatter_about(splits[0], (L, D), 1.0, 6.0, ((0, 16), (1, 2)))
    k_feat = scatter_about(splits[1], (L, D), 1.0, 6.0, ((0, 16), (1, 2)))
    v_feat = scatter_about(splits[2], (L, D), 1.0, 6.0, ((0, 16), (1, 2)))
    stream = scatter_about(splits[3], (L, D), 1.0, 6.0, ((0, 16), (1, 2)))
    filters = draw_filters(jax.random.fold_in(splits[6], 71), 0)
    w_out = bell_draw_with(splits[5], (D, D), D ** -0.5, 0.125, ((0, 2), (1, 16)), (0, 1, 16, 2.0))
    return dict(q_feat=q_feat, k_feat=k_feat, v_feat=v_feat, stream=stream, filters=filters, w_out=w_out)


def convolve_block(pair):
    signal, taps = pair
    length = signal.shape[1]
    spectrum = jnp.fft.rfft(signal, n=2 * length, axis=1) * jnp.fft.rfft(taps, n=2 * length, axis=1)
    return jnp.fft.irfft(spectrum, n=2 * length, axis=1)[:, :length]


def reference(q_feat, k_feat, v_feat, stream, filters, w_out):
    mixed = (k_feat.astype(jnp.float32) * v_feat.astype(jnp.float32)).astype(jnp.bfloat16)
    blocksize = math.gcd(D, 256)
    signal = mixed.astype(jnp.float32).T.reshape(D // blocksize, blocksize, L)
    taps = filters.astype(jnp.float32).reshape(D // blocksize, blocksize, L)
    conv = lax.map(convolve_block, (signal, taps)).reshape(D, L).T
    conv = lax.optimization_barrier(conv.astype(jnp.float32).astype(jnp.bfloat16))
    gated = (q_feat.astype(jnp.float32) * conv.astype(jnp.float32)).astype(jnp.bfloat16)
    projected = jnp.dot(gated, w_out, preferred_element_type=jnp.float32)
    return (stream.astype(jnp.float32) + projected).astype(jnp.bfloat16)
```

```python
import functools
import math

import jax
import jax.numpy as jnp
import numpy as np
from jax import lax
from jax.experimental import pallas as pl
from jax.experimental.pallas import tpu as pltpu
from jax.sharding import PartitionSpec as P

LANES = 128
GROUP = 16

def window_extent(total):
    chosen = 2
    for normalizing_multiplier in range(2, math.isqrt(total) + 1, 2):
        if total % normalizing_multiplier == 0:
            chosen = normalizing_multiplier
    return chosen


def make_tables(first, second, total):
    rows = jnp.arange(first, dtype=jnp.int32)
    half_rows = jnp.arange(first // 2, dtype=jnp.int32)
    columns = jnp.arange(second, dtype=jnp.int32)
    angle_one = (
        2.0 * math.pi / first * (rows[:, None] * half_rows[None, :] % first).astype(jnp.float32)
    )
    angle_two = (
        2.0 * math.pi / second * (columns[:, None] * columns[None, :] % second).astype(jnp.float32)
    )
    angle_twist = (
        2.0 * math.pi / total * (rows[:, None] * columns[None, :] % total).astype(jnp.float32)
    )
    return (
        jnp.cos(angle_one),
        jnp.sin(angle_one),
        jnp.cos(angle_two),
        jnp.sin(angle_two),
        jnp.cos(angle_twist),
        jnp.sin(angle_twist),
    )


def forward_transform(signal, tables, first, second):
    cosine_first, sin_one, cos_two, sin_two, cos_twist, sin_twist = tables
    chans = signal.shape[0]
    shaped = signal.reshape(chans, first // 2, second)
    highest = lax.Precision.HIGHEST
    real_a = jnp.einsum("kn,cnm->ckm", cosine_first, shaped, precision=highest)
    imaginary_left = -jnp.einsum("kn,cnm->ckm", sin_one, shaped, precision=highest)
    real_b = real_a * cos_twist + imaginary_left * sin_twist
    imag_b = imaginary_left * cos_twist - real_a * sin_twist
    real_x = jnp.einsum("ckn,nm->ckm", real_b, cos_two, precision=highest) + jnp.einsum(
        "ckn,nm->ckm", imag_b, sin_two, precision=highest
    )
    imag_x = jnp.einsum("ckn,nm->ckm", imag_b, cos_two, precision=highest) - jnp.einsum(
        "ckn,nm->ckm", real_b, sin_two, precision=highest
    )
    return (real_x, imag_x)


def inverse_transform(real_p, imag_p, tables, first, second):
    cosine_first, sin_one, cos_two, sin_two, cos_twist, sin_twist = tables
    highest = lax.Precision.HIGHEST
    real_d = jnp.einsum("ckn,nm->ckm", real_p, cos_two, precision=highest) - jnp.einsum(
        "ckn,nm->ckm", imag_p, sin_two, precision=highest
    )
    imag_d = jnp.einsum("ckn,nm->ckm", real_p, sin_two, precision=highest) + jnp.einsum(
        "ckn,nm->ckm", imag_p, cos_two, precision=highest
    )
    kernel_spectrum_real = real_d * cos_twist - imag_d * sin_twist
    imag_e = real_d * sin_twist + imag_d * cos_twist
    result = jnp.einsum(
        "kn,ckm->cnm", cosine_first, kernel_spectrum_real, precision=highest
    ) - jnp.einsum("kn,ckm->cnm", sin_one, imag_e, precision=highest)
    return result / (first * second)


def long_conv(mixed_cols, filters):
    chans, length = filters.shape
    total = 2 * length
    first = window_extent(total)
    second = total // first
    tables = make_tables(first, second, total)
    stacked = jnp.concatenate([mixed_cols.astype(jnp.float32), filters], axis=0)
    real_x, imag_x = forward_transform(stacked, tables, first, second)
    real_p = real_x[:chans] * real_x[chans:] - imag_x[:chans] * imag_x[chans:]
    imag_p = real_x[:chans] * imag_x[chans:] + imag_x[:chans] * real_x[chans:]
    result = inverse_transform(real_p, imag_p, tables, first, second)
    return result.reshape(chans, length)


def spectral_tables(length):
    total = 2 * length
    first = total // LANES
    slots = first // 2
    n_one = np.arange(slots)
    base = np.zeros((slots, 2, slots))
    for s in range(1, slots):
        angle = 2.0 * np.pi * (s * n_one % first) / first
        base[s, 0] = np.cos(angle)
        base[s, 1] = -np.sin(angle)
    base[0, 0] = 1.0
    base[0, 1] = 1.0 - 2.0 * (n_one % 2)
    outer = np.kron(base.reshape(first, slots), np.eye(GROUP))
    n_two = np.arange(LANES)
    k_two = np.arange(LANES)
    inner = np.zeros((slots, 2 * LANES, 2 * LANES))

    def wave(k_one, rows):
        turns = (first * rows[:, None] + k_one) * n_two[None, :] % total
        return np.exp(-2j * np.pi * turns / total)

    for s in range(1, slots):
        t = wave(s, k_two)
        inner[s] = np.block([[t.real, -t.imag], [t.imag, t.real]])
    half = LANES // 2
    zero = wave(0, k_two[:half])
    mid = wave(slots, k_two[:half])
    inner[0, :half, :LANES] = zero.real
    inner[0, half:LANES, LANES:] = mid.real
    inner[0, LANES : LANES + half, :LANES] = zero.imag
    inner[0, LANES + half :, LANES:] = mid.imag
    inner[0, LANES, :LANES] = 1.0 - 2.0 * (n_two % 2)
    cast = lambda a: np.ascontiguousarray(a).astype(jnp.bfloat16)
    return cast(outer), cast(outer.T), cast(inner), cast(inner.transpose(0, 2, 1))


def spectral_product(a, b, slot_zero):
    a_re, a_im = a[:LANES], a[LANES:]
    b_re, b_im = b[:LANES], b[LANES:]
    rr, ii = a_re * b_re, a_im * b_im
    p_re = rr - ii
    p_im = a_re * b_im + a_im * b_re
    if slot_zero:
        top = lax.broadcasted_iota(jnp.int32, p_re.shape, 0) == 0
        p_re = jnp.where(top, 0.5 * rr, p_re)
        p_im = jnp.where(top, 0.5 * ii, p_im)
    return jnp.concatenate([p_re, p_im], axis=0)


def mixer_kernel(
    peers,
    k_ref,
    v_ref,
    q_ref,
    taps_ref,
    outer_ref,
    outer_t_ref,
    inner_ref,
    inner_t_ref,
    gated_ref,
    sent,
    signal,
    result,
    returned,
    turned,
    spectrum,
    work,
    send_one,
    recv_one,
    send_two,
    recv_two,
):
    me = lax.axis_index("seq")
    rows = k_ref.shape[0]
    slots = signal.shape[0]
    per = slots // peers
    total = 2 * slots * LANES

    barrier = pltpu.get_barrier_semaphore()
    for i in range(1, peers):
        pl.semaphore_signal(
            barrier,
            inc=1,
            device_id={"seq": lax.rem(me + i, peers)},
            device_id_type=pl.DeviceIdType.MESH,
        )

    def mix(p, carry):
        cols = pl.ds(pl.multiple_of(p * LANES, LANES), LANES)
        product = k_ref[:, cols].astype(jnp.float32) * v_ref[:, cols].astype(jnp.float32)
        sent[p] = product.astype(jnp.bfloat16).reshape(per, LANES, LANES)
        return carry

    lax.fori_loop(0, peers, mix, 0)
    pl.semaphore_wait(barrier, peers - 1)

    first_copies = []
    for i in range(1, peers):
        target = lax.rem(me + i, peers)
        copy = pltpu.make_async_remote_copy(
            src_ref=sent.at[target],
            dst_ref=signal.at[pl.ds(me * per, per)],
            send_sem=send_one.at[i],
            recv_sem=recv_one.at[i],
            device_id={"seq": target},
            device_id_type=pl.DeviceIdType.MESH,
        )
        copy.start()
        first_copies.append(copy)
    signal[pl.ds(me * per, per)] = sent[me]

    def outer_stage(source):
        def step(g, carry):
            lo = pl.ds(pl.multiple_of(g * 2 * GROUP, 2 * GROUP), GROUP)
            hi = pl.ds(pl.multiple_of(g * 2 * GROUP + GROUP, GROUP), GROUP)
            block = jnp.concatenate(
                [
                    source[:, lo, :].reshape(slots * GROUP, LANES),
                    source[:, hi, :].reshape(slots * GROUP, LANES),
                ],
                axis=1,
            )
            y = jnp.dot(outer_ref[...], block, preferred_element_type=jnp.float32)
            y = y.astype(jnp.bfloat16)
            work[:, :, lo, :] = y[:, :LANES].reshape(slots, 2, GROUP, LANES)
            work[:, :, hi, :] = y[:, LANES:].reshape(slots, 2, GROUP, LANES)
            return carry

        lax.fori_loop(0, LANES // (2 * GROUP), step, 0)

    def inner_forward(s):
        return jnp.dot(
            inner_ref[s],
            work[s].reshape(2 * LANES, LANES),
            preferred_element_type=jnp.float32,
        )

    def turn(n, carry):
        cols = pl.ds(pl.multiple_of(n * LANES, LANES), LANES)
        turned[n] = taps_ref[:, cols].T.astype(jnp.bfloat16)
        return carry

    lax.fori_loop(0, slots, turn, 0)
    outer_stage(turned)

    def tap_step(s, carry):
        spectrum[s] = inner_forward(s)
        return carry

    lax.fori_loop(0, slots, tap_step, 0, unroll=2)

    for copy in first_copies:
        copy.wait_recv()
    outer_stage(signal)

    def middle(s, slot_zero):
        p = spectral_product(inner_forward(s), spectrum[s], slot_zero)
        q = jnp.dot(inner_t_ref[s], p.astype(jnp.bfloat16), preferred_element_type=jnp.float32)
        work[s] = q.astype(jnp.bfloat16).reshape(2, LANES, LANES)

    middle(0, True)

    def middle_step(s, carry):
        middle(s, False)
        return carry

    lax.fori_loop(1, slots, middle_step, 0, unroll=2)

    def outer_back(g, carry):
        lo = pl.ds(pl.multiple_of(g * 2 * GROUP, 2 * GROUP), GROUP)
        hi = pl.ds(pl.multiple_of(g * 2 * GROUP + GROUP, GROUP), GROUP)
        block = jnp.concatenate(
            [
                work[:, :, lo, :].reshape(2 * slots * GROUP, LANES),
                work[:, :, hi, :].reshape(2 * slots * GROUP, LANES),
            ],
            axis=1,
        )
        y = jnp.dot(outer_t_ref[...], block, preferred_element_type=jnp.float32)
        y = (y * (2.0 / total)).astype(jnp.bfloat16)
        result[:, lo, :] = y[:, :LANES].reshape(slots, GROUP, LANES)
        result[:, hi, :] = y[:, LANES:].reshape(slots, GROUP, LANES)
        return carry

    lax.fori_loop(0, LANES // (2 * GROUP), outer_back, 0)

    second_copies = []
    for i in range(1, peers):
        target = lax.rem(me + i, peers)
        copy = pltpu.make_async_remote_copy(
            src_ref=result.at[pl.ds(target * per, per)],
            dst_ref=returned.at[me],
            send_sem=send_two.at[i],
            recv_sem=recv_two.at[i],
            device_id={"seq": target},
            device_id_type=pl.DeviceIdType.MESH,
        )
        copy.start()
        second_copies.append(copy)

    def gate(p, block):
        cols = pl.ds(pl.multiple_of(p * LANES, LANES), LANES)
        conv = block.reshape(rows, LANES).astype(jnp.float32)
        gated_ref[:, cols] = (q_ref[:, cols].astype(jnp.float32) * conv).astype(jnp.bfloat16)

    gate(me, result[pl.ds(me * per, per)])
    for i, copy in enumerate(second_copies, 1):
        copy.wait_recv()
        source = lax.rem(me + peers - i, peers)
        gate(source, returned[source])
    for copy in first_copies + second_copies:
        copy.wait_send()


def gated_mixer(q_feat, k_feat, v_feat, filters, peers):
    rows, columns = q_feat.shape
    chans, length = filters.shape
    slots = length // LANES
    per = rows // LANES
    tables = spectral_tables(length)
    vmem = pl.BlockSpec(memory_space=pltpu.VMEM)
    bf16 = jnp.bfloat16
    return pl.pallas_call(
        functools.partial(mixer_kernel, peers),
        out_shape=jax.ShapeDtypeStruct((rows, columns), bf16),
        in_specs=[vmem] * 8,
        out_specs=vmem,
        scratch_shapes=[
            pltpu.VMEM((peers, per, LANES, LANES), bf16),
            pltpu.VMEM((slots, LANES, LANES), bf16),
            pltpu.VMEM((slots, LANES, LANES), bf16),
            pltpu.VMEM((peers, per, LANES, LANES), bf16),
            pltpu.VMEM((slots, LANES, LANES), bf16),
            pltpu.VMEM((slots, 2 * LANES, LANES), jnp.float32),
            pltpu.VMEM((slots, 2, LANES, LANES), bf16),
            pltpu.SemaphoreType.DMA((peers,)),
            pltpu.SemaphoreType.DMA((peers,)),
            pltpu.SemaphoreType.DMA((peers,)),
            pltpu.SemaphoreType.DMA((peers,)),
        ],
        compiler_params=pltpu.CompilerParams(
            collective_id=0, has_side_effects=True, vmem_limit_bytes=48 * 1024 * 1024
        ),
        cost_estimate=pl.CostEstimate(
            flops=40 * 1024 * 1024 * slots * chans // 8,
            bytes_accessed=16 * 1024 * 1024,
            transcendentals=0,
        ),
    )(k_feat, v_feat, q_feat, filters, *[jnp.asarray(t) for t in tables])


def gated_features(q_feat, k_feat, v_feat, filters):
    peers = lax.axis_size("seq")
    if filters.shape[0] == LANES and q_feat.shape[0] % LANES == 0:
        return gated_mixer(q_feat, k_feat, v_feat, filters, peers)
    mixed = (k_feat.astype(jnp.float32) * v_feat.astype(jnp.float32)).astype(jnp.bfloat16)
    sent_mixed = lax.all_to_all(mixed.T, "seq", split_axis=0, concat_axis=1, tiled=True)
    conv_out = long_conv(sent_mixed, filters).astype(jnp.bfloat16)
    returned_output = lax.all_to_all(conv_out, "seq", split_axis=1, concat_axis=0, tiled=True)
    return (q_feat.astype(jnp.float32) * returned_output.T.astype(jnp.float32)).astype(
        jnp.bfloat16
    )


def local(q_feat, k_feat, v_feat, stream, filters, w_out):
    gated = gated_features(q_feat, k_feat, v_feat, filters)
    terms = jnp.dot(
        gated, lax.all_gather(w_out, "seq", axis=1, tiled=True), preferred_element_type=jnp.float32
    )
    accumulated_total = lax.psum_scatter(
        terms.astype(jnp.bfloat16), "tp", scatter_dimension=1, tiled=True
    ).astype(jnp.float32)
    return (stream.astype(jnp.float32) + accumulated_total).astype(jnp.bfloat16)


def solution(mesh):
    return jax.shard_map(
        local,
        mesh=mesh,
        in_specs=(
            P("seq", "tp"),
            P("seq", "tp"),
            P("seq", "tp"),
            P("seq", "tp"),
            P(("tp", "seq"), None),
            P("tp", "seq"),
        ),
        out_specs=P("seq", "tp"),
        check_vma=False,
    )
```

```python
import functools
import math

import jax
import jax.numpy as jnp
import numpy as np
from jax import lax
from jax.experimental import pallas as pl
from jax.experimental.pallas import tpu as pltpu
from jax.sharding import PartitionSpec as P

LANES = 128
GROUP = 16

def window_extent(total):
    chosen = 2
    for normalizing_multiplier in range(2, math.isqrt(total) + 1, 2):
        if total % normalizing_multiplier == 0:
            chosen = normalizing_multiplier
    return chosen


def make_tables(first, second, total):
    rows = jnp.arange(first, dtype=jnp.int32)
    half_rows = jnp.arange(first // 2, dtype=jnp.int32)
    columns = jnp.arange(second, dtype=jnp.int32)
    angle_one = (
        2.0 * math.pi / first * (rows[:, None] * half_rows[None, :] % first).astype(jnp.float32)
    )
    angle_two = (
        2.0 * math.pi / second * (columns[:, None] * columns[None, :] % second).astype(jnp.float32)
    )
    angle_twist = (
        2.0 * math.pi / total * (rows[:, None] * columns[None, :] % total).astype(jnp.float32)
    )
    return (
        jnp.cos(angle_one),
        jnp.sin(angle_one),
        jnp.cos(angle_two),
        jnp.sin(angle_two),
        jnp.cos(angle_twist),
        jnp.sin(angle_twist),
    )


def forward_transform(signal, tables, first, second):
    cosine_first, sin_one, cos_two, sin_two, cos_twist, sin_twist = tables
    chans = signal.shape[0]
    shaped = signal.reshape(chans, first // 2, second)
    highest = lax.Precision.HIGHEST
    real_a = jnp.einsum("kn,cnm->ckm", cosine_first, shaped, precision=highest)
    imaginary_left = -jnp.einsum("kn,cnm->ckm", sin_one, shaped, precision=highest)
    real_b = real_a * cos_twist + imaginary_left * sin_twist
    imag_b = imaginary_left * cos_twist - real_a * sin_twist
    real_x = jnp.einsum("ckn,nm->ckm", real_b, cos_two, precision=highest) + jnp.einsum(
        "ckn,nm->ckm", imag_b, sin_two, precision=highest
    )
    imag_x = jnp.einsum("ckn,nm->ckm", imag_b, cos_two, precision=highest) - jnp.einsum(
        "ckn,nm->ckm", real_b, sin_two, precision=highest
    )
    return (real_x, imag_x)


def inverse_transform(real_p, imag_p, tables, first, second):
    cosine_first, sin_one, cos_two, sin_two, cos_twist, sin_twist = tables
    highest = lax.Precision.HIGHEST
    real_d = jnp.einsum("ckn,nm->ckm", real_p, cos_two, precision=highest) - jnp.einsum(
        "ckn,nm->ckm", imag_p, sin_two, precision=highest
    )
    imag_d = jnp.einsum("ckn,nm->ckm", real_p, sin_two, precision=highest) + jnp.einsum(
        "ckn,nm->ckm", imag_p, cos_two, precision=highest
    )
    kernel_spectrum_real = real_d * cos_twist - imag_d * sin_twist
    imag_e = real_d * sin_twist + imag_d * cos_twist
    result = jnp.einsum(
        "kn,ckm->cnm", cosine_first, kernel_spectrum_real, precision=highest
    ) - jnp.einsum("kn,ckm->cnm", sin_one, imag_e, precision=highest)
    return result / (first * second)


def long_conv(mixed_cols, filters):
    chans, length = filters.shape
    total = 2 * length
    first = window_extent(total)
    second = total // first
    tables = make_tables(first, second, total)
    stacked = jnp.concatenate([mixed_cols.astype(jnp.float32), filters], axis=0)
    real_x, imag_x = forward_transform(stacked, tables, first, second)
    real_p = real_x[:chans] * real_x[chans:] - imag_x[:chans] * imag_x[chans:]
    imag_p = real_x[:chans] * imag_x[chans:] + imag_x[:chans] * real_x[chans:]
    result = inverse_transform(real_p, imag_p, tables, first, second)
    return result.reshape(chans, length)


def spectral_tables(length):
    total = 2 * length
    first = total // LANES
    slots = first // 2
    n_one = np.arange(slots)
    base = np.zeros((slots, 2, slots))
    for s in range(1, slots):
        angle = 2.0 * np.pi * (s * n_one % first) / first
        base[s, 0] = np.cos(angle)
        base[s, 1] = -np.sin(angle)
    base[0, 0] = 1.0
    base[0, 1] = 1.0 - 2.0 * (n_one % 2)
    outer = np.kron(base.reshape(first, slots), np.eye(GROUP))
    n_two = np.arange(LANES)
    k_two = np.arange(LANES)
    inner = np.zeros((slots, 2 * LANES, 2 * LANES))

    def wave(k_one, rows):
        turns = (first * rows[:, None] + k_one) * n_two[None, :] % total
        return np.exp(-2j * np.pi * turns / total)

    for s in range(1, slots):
        t = wave(s, k_two)
        inner[s] = np.block([[t.real, -t.imag], [t.imag, t.real]])
    half = LANES // 2
    zero = wave(0, k_two[:half])
    mid = wave(slots, k_two[:half])
    inner[0, :half, :LANES] = zero.real
    inner[0, half:LANES, LANES:] = mid.real
    inner[0, LANES : LANES + half, :LANES] = zero.imag
    inner[0, LANES + half :, LANES:] = mid.imag
    inner[0, LANES, :LANES] = 1.0 - 2.0 * (n_two % 2)
    cast = lambda a: np.ascontiguousarray(a).astype(jnp.bfloat16)
    return cast(outer), cast(outer.T), cast(inner), cast(inner.transpose(0, 2, 1))


def spectral_product(a, b, slot_zero):
    a_re, a_im = a[:LANES], a[LANES:]
    b_re, b_im = b[:LANES], b[LANES:]
    rr, ii = a_re * b_re, a_im * b_im
    p_re = rr - ii
    p_im = a_re * b_im + a_im * b_re
    if slot_zero:
        top = lax.broadcasted_iota(jnp.int32, p_re.shape, 0) == 0
        p_re = jnp.where(top, 0.5 * rr, p_re)
        p_im = jnp.where(top, 0.5 * ii, p_im)
    return jnp.concatenate([p_re, p_im], axis=0)


def mixer_kernel(
    peers,
    k_ref,
    v_ref,
    q_hbm,
    stream_hbm,
    taps_hbm,
    weights_hbm,
    outer_hbm,
    outer_t_hbm,
    inner_hbm,
    inner_t_hbm,
    out_ref,
    q_ref,
    stream_ref,
    taps_ref,
    outer_ref,
    outer_t_ref,
    inner_ref,
    inner_t_ref,
    sent,
    signal,
    result,
    returned,
    turned,
    spectrum,
    work,
    gated,
    weights,
    kept,
    shares,
    arrived,
    load_sem,
    send_one,
    recv_one,
    send_two,
    recv_two,
    send_weight,
    recv_weight,
    send_share,
    recv_share,
):
    me = lax.axis_index("seq")
    tp = lax.axis_index("tp")
    rows = k_ref.shape[0]
    slots = signal.shape[0]
    per = slots // peers
    total = 2 * slots * LANES
    mesh_ids = pl.DeviceIdType.MESH
    depth = peers // 4
    half = peers // 2
    layer, side, core = me // 4, (me // 2) % 2, me % 2

    loads = [
        pltpu.make_async_copy(source, target, load_sem.at[i])
        for i, (source, target) in enumerate(
            [
                (weights_hbm, weights.at[me]),
                (taps_hbm, taps_ref),
                (outer_hbm, outer_ref),
                (inner_hbm, inner_ref),
                (inner_t_hbm, inner_t_ref),
                (outer_t_hbm, outer_t_ref),
                (q_hbm, q_ref),
                (stream_hbm, stream_ref),
            ]
        )
    ]
    for load in loads:
        load.start()

    def block_at(zz, xx, cc):
        return (zz * 2 + xx) * 2 + cc

    def weight_copy(block, target, way):
        return pltpu.make_async_remote_copy(
            src_ref=weights.at[block],
            dst_ref=weights.at[block],
            send_sem=send_weight.at[block, way],
            recv_sem=recv_weight.at[block],
            device_id={"seq": target},
            device_id_type=mesh_ids,
        )

    to_core = block_at(layer, side, 1 - core)
    to_side = block_at(layer, 1 - side, core)

    def act(copy, sending):
        if sending:
            copy.start()
        else:
            copy.wait_send()

    def spread(block, sending, up, down):
        if up:

            @pl.when(layer + 1 < depth)
            def _():
                act(weight_copy(block, me + 4, 2), sending)

        if down:

            @pl.when(layer > 0)
            def _():
                act(weight_copy(block, me - 4, 3), sending)

        act(weight_copy(block, to_side, 1), sending)
        act(weight_copy(block, to_core, 0), sending)

    def arrive(block):
        weight_copy(block, to_core, 0).wait_recv()

    def at_distance(d, body):
        for sign in (-1, 1) if d else (1,):
            zz = layer + sign * d

            @pl.when((zz >= 0) & (zz < depth))
            def _():
                body(zz, sign)

    def from_layer(d):
        if d >= depth:
            return

        def body(zz, sign):
            block = block_at(zz, side, core)
            arrive(block)
            spread(block, True, sign < 0, sign > 0)

        at_distance(d, body)

    def from_side(d):
        if d >= depth:
            return

        def body(zz, sign):
            block = block_at(zz, 1 - side, core)
            arrive(block)
            weight_copy(block, to_core, 0).start()

        at_distance(d, body)

    def share_copy(b):
        return pltpu.make_async_remote_copy(
            src_ref=shares.at[b],
            dst_ref=arrived.at[b],
            send_sem=send_share.at[b],
            recv_sem=recv_share.at[b],
            device_id={"tp": 1 - tp},
            device_id_type=mesh_ids,
        )

    def project(d):
        def body(zz, sign):
            for xx in (0, 1):
                arrive(block_at(zz, xx, 1 - core))

            def step(i, carry):
                block = zz * 4 + i
                terms = jnp.dot(gated[...], weights[block], preferred_element_type=jnp.float32)
                b = block % half

                @pl.when(block // half == tp)
                def _():
                    kept[b] = terms

                @pl.when(block // half != tp)
                def _():
                    shares[b] = terms.astype(jnp.bfloat16)
                    share_copy(b).start()

                return carry

            lax.fori_loop(0, 4, step, 0)

        if d < depth:
            at_distance(d, body)

    barrier = pltpu.get_barrier_semaphore()
    for i in range(1, peers):
        pl.semaphore_signal(
            barrier,
            inc=1,
            device_id={"seq": lax.rem(me + i, peers)},
            device_id_type=mesh_ids,
        )
    pl.semaphore_signal(barrier, inc=1, device_id={"tp": 1 - tp}, device_id_type=mesh_ids)

    def mix(p, carry):
        cols = pl.ds(pl.multiple_of(p * LANES, LANES), LANES)
        product = k_ref[:, cols].astype(jnp.float32) * v_ref[:, cols].astype(jnp.float32)
        sent[p] = product.astype(jnp.bfloat16).reshape(per, LANES, LANES)
        return carry

    lax.fori_loop(0, peers, mix, 0)
    pl.semaphore_wait(barrier, peers)

    first_copies = []
    for i in range(1, peers):
        target = lax.rem(me + i, peers)
        copy = pltpu.make_async_remote_copy(
            src_ref=sent.at[target],
            dst_ref=signal.at[pl.ds(me * per, per)],
            send_sem=send_one.at[i],
            recv_sem=recv_one.at[i],
            device_id={"seq": target},
            device_id_type=mesh_ids,
        )
        copy.start()
        first_copies.append(copy)
    signal[pl.ds(me * per, per)] = sent[me]
    loads[0].wait()
    spread(me, True, True, True)

    def outer_stage(source):
        def step(g, carry):
            lo = pl.ds(pl.multiple_of(g * 2 * GROUP, 2 * GROUP), GROUP)
            hi = pl.ds(pl.multiple_of(g * 2 * GROUP + GROUP, GROUP), GROUP)
            block = jnp.concatenate(
                [
                    source[:, lo, :].reshape(slots * GROUP, LANES),
                    source[:, hi, :].reshape(slots * GROUP, LANES),
                ],
                axis=1,
            )
            y = jnp.dot(outer_ref[...], block, preferred_element_type=jnp.float32)
            y = y.astype(jnp.bfloat16)
            work[:, :, lo, :] = y[:, :LANES].reshape(slots, 2, GROUP, LANES)
            work[:, :, hi, :] = y[:, LANES:].reshape(slots, 2, GROUP, LANES)
            return carry

        lax.fori_loop(0, LANES // (2 * GROUP), step, 0)

    def inner_forward(s):
        return jnp.dot(
            inner_ref[s],
            work[s].reshape(2 * LANES, LANES),
            preferred_element_type=jnp.float32,
        )

    def turn(n, carry):
        cols = pl.ds(pl.multiple_of(n * LANES, LANES), LANES)
        turned[n] = taps_ref[:, cols].T.astype(jnp.bfloat16)
        return carry

    loads[1].wait()
    lax.fori_loop(0, slots, turn, 0)
    loads[2].wait()
    outer_stage(turned)
    loads[3].wait()

    def tap_step(s, carry):
        spectrum[s] = inner_forward(s)
        return carry

    lax.fori_loop(0, slots, tap_step, 0, unroll=2)

    for copy in first_copies:
        copy.wait_recv()
    outer_stage(signal)
    from_layer(1)
    loads[4].wait()

    def middle(s, slot_zero):
        p = spectral_product(inner_forward(s), spectrum[s], slot_zero)
        q = jnp.dot(inner_t_ref[s], p.astype(jnp.bfloat16), preferred_element_type=jnp.float32)
        work[s] = q.astype(jnp.bfloat16).reshape(2, LANES, LANES)

    middle(0, True)

    def middle_step(s, carry):
        middle(s, False)
        return carry

    lax.fori_loop(1, slots, middle_step, 0, unroll=2)

    loads[5].wait()

    def outer_back(g, carry):
        lo = pl.ds(pl.multiple_of(g * 2 * GROUP, 2 * GROUP), GROUP)
        hi = pl.ds(pl.multiple_of(g * 2 * GROUP + GROUP, GROUP), GROUP)
        block = jnp.concatenate(
            [
                work[:, :, lo, :].reshape(2 * slots * GROUP, LANES),
                work[:, :, hi, :].reshape(2 * slots * GROUP, LANES),
            ],
            axis=1,
        )
        y = jnp.dot(outer_t_ref[...], block, preferred_element_type=jnp.float32)
        y = (y * (2.0 / total)).astype(jnp.bfloat16)
        result[:, lo, :] = y[:, :LANES].reshape(slots, GROUP, LANES)
        result[:, hi, :] = y[:, LANES:].reshape(slots, GROUP, LANES)
        return carry

    lax.fori_loop(0, LANES // (2 * GROUP), outer_back, 0)

    second_copies = []
    for i in range(1, peers):
        target = lax.rem(me + i, peers)
        copy = pltpu.make_async_remote_copy(
            src_ref=result.at[pl.ds(target * per, per)],
            dst_ref=returned.at[me],
            send_sem=send_two.at[i],
            recv_sem=recv_two.at[i],
            device_id={"seq": target},
            device_id_type=mesh_ids,
        )
        copy.start()
        second_copies.append(copy)
    from_side(0)
    from_layer(2)
    from_side(1)
    loads[6].wait()

    def gate(p, block):
        cols = pl.ds(pl.multiple_of(p * LANES, LANES), LANES)
        conv = block.reshape(rows, LANES).astype(jnp.float32)
        gated[:, cols] = (q_ref[:, cols].astype(jnp.float32) * conv).astype(jnp.bfloat16)

    gate(me, result[pl.ds(me * per, per)])
    for i, copy in enumerate(second_copies, 1):
        copy.wait_recv()
        source = lax.rem(me + peers - i, peers)
        gate(source, returned[source])
    project(0)
    from_layer(3)
    from_side(2)
    project(1)
    project(2)
    for d in range(3, depth):
        if d > 3:
            from_layer(d)
        from_side(d)
        project(d)

    loads[7].wait()
    width = kept.shape[2]

    def finish(b, carry):
        share_copy(b).wait_recv()
        cols = pl.ds(pl.multiple_of(b * width, width), width)
        added = kept[b] + arrived[b].astype(jnp.float32)
        out_ref[:, cols] = (stream_ref[:, cols].astype(jnp.float32) + added).astype(jnp.bfloat16)
        return carry

    lax.fori_loop(0, half, finish, 0)

    for copy in first_copies + second_copies:
        copy.wait_send()
    spread(me, False, True, True)
    for d in range(depth):

        def settle(zz, sign):
            if d:
                spread(block_at(zz, side, core), False, sign < 0, sign > 0)
            weight_copy(block_at(zz, 1 - side, core), to_core, 0).wait_send()

        at_distance(d, settle)

    def sent_share(b, carry):
        share_copy(b).wait_send()
        return carry

    lax.fori_loop(0, half, sent_share, 0)


def fused_mixer(q_feat, k_feat, v_feat, stream, filters, w_out, peers):
    rows, columns = q_feat.shape
    chans, length = filters.shape
    slots = length // LANES
    per = rows // LANES
    tables = spectral_tables(length)
    vmem = pl.BlockSpec(memory_space=pltpu.VMEM)
    anywhere = pl.BlockSpec(memory_space=pl.ANY)
    bf16 = jnp.bfloat16
    depth, width = w_out.shape
    half = peers // 2
    dma = pltpu.SemaphoreType.DMA
    return pl.pallas_call(
        functools.partial(mixer_kernel, peers),
        out_shape=jax.ShapeDtypeStruct((rows, columns), bf16),
        in_specs=[vmem] * 2 + [anywhere] * 8,
        out_specs=vmem,
        scratch_shapes=[
            pltpu.VMEM((rows, columns), bf16),
            pltpu.VMEM((rows, columns), bf16),
            pltpu.VMEM((chans, length), jnp.float32),
        ]
        + [pltpu.VMEM(t.shape, bf16) for t in tables]
        + [
            pltpu.VMEM((peers, per, LANES, LANES), bf16),
            pltpu.VMEM((slots, LANES, LANES), bf16),
            pltpu.VMEM((slots, LANES, LANES), bf16),
            pltpu.VMEM((peers, per, LANES, LANES), bf16),
            pltpu.VMEM((slots, LANES, LANES), bf16),
            pltpu.VMEM((slots, 2 * LANES, LANES), jnp.float32),
            pltpu.VMEM((slots, 2, LANES, LANES), bf16),
            pltpu.VMEM((rows, columns), bf16),
            pltpu.VMEM((peers, depth, width), bf16),
            pltpu.VMEM((half, rows, width), jnp.float32),
            pltpu.VMEM((half, rows, width), bf16),
            pltpu.VMEM((half, rows, width), bf16),
            dma((8,)),
            dma((peers,)),
            dma((peers,)),
            dma((peers,)),
            dma((peers,)),
            dma((peers, 4)),
            dma((peers,)),
            dma((half,)),
            dma((half,)),
        ],
        compiler_params=pltpu.CompilerParams(
            collective_id=0, has_side_effects=True, vmem_limit_bytes=58 * 1024 * 1024
        ),
        cost_estimate=pl.CostEstimate(
            flops=2 * rows * depth * width * peers,
            bytes_accessed=16 * 1024 * 1024,
            transcendentals=0,
        ),
    )(k_feat, v_feat, q_feat, stream, filters, w_out, *[jnp.asarray(t) for t in tables])


def gated_features(q_feat, k_feat, v_feat, filters):
    mixed = (k_feat.astype(jnp.float32) * v_feat.astype(jnp.float32)).astype(jnp.bfloat16)
    sent_mixed = lax.all_to_all(mixed.T, "seq", split_axis=0, concat_axis=1, tiled=True)
    conv_out = long_conv(sent_mixed, filters).astype(jnp.bfloat16)
    returned_output = lax.all_to_all(conv_out, "seq", split_axis=1, concat_axis=0, tiled=True)
    return (q_feat.astype(jnp.float32) * returned_output.T.astype(jnp.float32)).astype(
        jnp.bfloat16
    )


def local(q_feat, k_feat, v_feat, stream, filters, w_out):
    peers = lax.axis_size("seq")
    if (
        filters.shape[0] == LANES
        and q_feat.shape[0] % LANES == 0
        and peers % 4 == 0
        and lax.axis_size("tp") == 2
        and w_out.shape[1] % LANES == 0
    ):
        return fused_mixer(q_feat, k_feat, v_feat, stream, filters, w_out, peers)
    gated = gated_features(q_feat, k_feat, v_feat, filters)
    terms = jnp.dot(
        gated, lax.all_gather(w_out, "seq", axis=1, tiled=True), preferred_element_type=jnp.float32
    )
    accumulated_total = lax.psum_scatter(
        terms.astype(jnp.bfloat16), "tp", scatter_dimension=1, tiled=True
    ).astype(jnp.float32)
    return (stream.astype(jnp.float32) + accumulated_total).astype(jnp.bfloat16)


def solution(mesh):
    return jax.shard_map(
        local,
        mesh=mesh,
        in_specs=(
            P("seq", "tp"),
            P("seq", "tp"),
            P("seq", "tp"),
            P("seq", "tp"),
            P(("tp", "seq"), None),
            P("tp", "seq"),
        ),
        out_specs=P("seq", "tp"),
        check_vma=False,
    )
```

```python
import functools
import math

import jax
import jax.numpy as jnp
import numpy as np
from jax import lax
from jax.experimental import pallas as pl
from jax.experimental.pallas import tpu as pltpu
from jax.sharding import PartitionSpec as P

LANES = 128
GROUP = 16
PIECES = 4

def window_extent(total):
    chosen = 2
    for normalizing_multiplier in range(2, math.isqrt(total) + 1, 2):
        if total % normalizing_multiplier == 0:
            chosen = normalizing_multiplier
    return chosen


def make_tables(first, second, total):
    rows = jnp.arange(first, dtype=jnp.int32)
    half_rows = jnp.arange(first // 2, dtype=jnp.int32)
    columns = jnp.arange(second, dtype=jnp.int32)
    angle_one = (
        2.0 * math.pi / first * (rows[:, None] * half_rows[None, :] % first).astype(jnp.float32)
    )
    angle_two = (
        2.0 * math.pi / second * (columns[:, None] * columns[None, :] % second).astype(jnp.float32)
    )
    angle_twist = (
        2.0 * math.pi / total * (rows[:, None] * columns[None, :] % total).astype(jnp.float32)
    )
    return (
        jnp.cos(angle_one),
        jnp.sin(angle_one),
        jnp.cos(angle_two),
        jnp.sin(angle_two),
        jnp.cos(angle_twist),
        jnp.sin(angle_twist),
    )


def forward_transform(signal, tables, first, second):
    cosine_first, sin_one, cos_two, sin_two, cos_twist, sin_twist = tables
    chans = signal.shape[0]
    shaped = signal.reshape(chans, first // 2, second)
    highest = lax.Precision.HIGHEST
    real_a = jnp.einsum("kn,cnm->ckm", cosine_first, shaped, precision=highest)
    imaginary_left = -jnp.einsum("kn,cnm->ckm", sin_one, shaped, precision=highest)
    real_b = real_a * cos_twist + imaginary_left * sin_twist
    imag_b = imaginary_left * cos_twist - real_a * sin_twist
    real_x = jnp.einsum("ckn,nm->ckm", real_b, cos_two, precision=highest) + jnp.einsum(
        "ckn,nm->ckm", imag_b, sin_two, precision=highest
    )
    imag_x = jnp.einsum("ckn,nm->ckm", imag_b, cos_two, precision=highest) - jnp.einsum(
        "ckn,nm->ckm", real_b, sin_two, precision=highest
    )
    return (real_x, imag_x)


def inverse_transform(real_p, imag_p, tables, first, second):
    cosine_first, sin_one, cos_two, sin_two, cos_twist, sin_twist = tables
    highest = lax.Precision.HIGHEST
    real_d = jnp.einsum("ckn,nm->ckm", real_p, cos_two, precision=highest) - jnp.einsum(
        "ckn,nm->ckm", imag_p, sin_two, precision=highest
    )
    imag_d = jnp.einsum("ckn,nm->ckm", real_p, sin_two, precision=highest) + jnp.einsum(
        "ckn,nm->ckm", imag_p, cos_two, precision=highest
    )
    kernel_spectrum_real = real_d * cos_twist - imag_d * sin_twist
    imag_e = real_d * sin_twist + imag_d * cos_twist
    result = jnp.einsum(
        "kn,ckm->cnm", cosine_first, kernel_spectrum_real, precision=highest
    ) - jnp.einsum("kn,ckm->cnm", sin_one, imag_e, precision=highest)
    return result / (first * second)


def long_conv(mixed_cols, filters):
    chans, length = filters.shape
    total = 2 * length
    first = window_extent(total)
    second = total // first
    tables = make_tables(first, second, total)
    stacked = jnp.concatenate([mixed_cols.astype(jnp.float32), filters], axis=0)
    real_x, imag_x = forward_transform(stacked, tables, first, second)
    real_p = real_x[:chans] * real_x[chans:] - imag_x[:chans] * imag_x[chans:]
    imag_p = real_x[:chans] * imag_x[chans:] + imag_x[:chans] * real_x[chans:]
    result = inverse_transform(real_p, imag_p, tables, first, second)
    return result.reshape(chans, length)


def spectral_tables(length):
    total = 2 * length
    first = total // LANES
    slots = first // 2
    n_one = np.arange(slots)
    base = np.zeros((slots, 2, slots))
    for s in range(1, slots):
        angle = 2.0 * np.pi * (s * n_one % first) / first
        base[s, 0] = np.cos(angle)
        base[s, 1] = -np.sin(angle)
    base[0, 0] = 1.0
    base[0, 1] = 1.0 - 2.0 * (n_one % 2)
    outer = np.kron(base.reshape(first, slots), np.eye(GROUP))
    n_two = np.arange(LANES)
    k_two = np.arange(LANES)
    inner = np.zeros((slots, 2 * LANES, 2 * LANES))

    def wave(k_one, rows):
        turns = (first * rows[:, None] + k_one) * n_two[None, :] % total
        return np.exp(-2j * np.pi * turns / total)

    for s in range(1, slots):
        t = wave(s, k_two)
        inner[s] = np.block([[t.real, -t.imag], [t.imag, t.real]])
    half = LANES // 2
    zero = wave(0, k_two[:half])
    mid = wave(slots, k_two[:half])
    inner[0, :half, :LANES] = zero.real
    inner[0, half:LANES, LANES:] = mid.real
    inner[0, LANES : LANES + half, :LANES] = zero.imag
    inner[0, LANES + half :, LANES:] = mid.imag
    inner[0, LANES, :LANES] = 1.0 - 2.0 * (n_two % 2)
    cast = lambda a: np.ascontiguousarray(a).astype(jnp.bfloat16)
    return cast(outer), cast(outer.T), cast(inner), cast(inner.transpose(0, 2, 1))


def spectral_product(a, b, slot_zero):
    a_re, a_im = a[:LANES], a[LANES:]
    b_re, b_im = b[:LANES], b[LANES:]
    rr, ii = a_re * b_re, a_im * b_im
    p_re = rr - ii
    p_im = a_re * b_im + a_im * b_re
    if slot_zero:
        top = lax.broadcasted_iota(jnp.int32, p_re.shape, 0) == 0
        p_re = jnp.where(top, 0.5 * rr, p_re)
        p_im = jnp.where(top, 0.5 * ii, p_im)
    return jnp.concatenate([p_re, p_im], axis=0)


def mixer_kernel(
    peers,
    k_ref,
    v_ref,
    q_hbm,
    stream_hbm,
    taps_hbm,
    weights_hbm,
    outer_hbm,
    outer_t_hbm,
    inner_hbm,
    inner_t_hbm,
    out_ref,
    q_ref,
    stream_ref,
    taps_ref,
    outer_ref,
    outer_t_ref,
    inner_ref,
    inner_t_ref,
    sent,
    signal,
    result,
    returned,
    turned,
    spectrum,
    work,
    gated,
    weights,
    kept,
    shares,
    arrived,
    load_sem,
    send_one,
    recv_one,
    send_two,
    recv_two,
    send_weight,
    recv_weight,
    send_share,
    recv_share,
):
    me = lax.axis_index("seq")
    tp = lax.axis_index("tp")
    rows = k_ref.shape[0]
    slots = signal.shape[0]
    per = slots // peers
    total = 2 * slots * LANES
    mesh_ids = pl.DeviceIdType.MESH
    depth = peers // 4
    half = peers // 2
    layer, side, core = me // 4, (me // 2) % 2, me % 2

    loads = [
        pltpu.make_async_copy(source, target, load_sem.at[i])
        for i, (source, target) in enumerate(
            [
                (weights_hbm, weights.at[me]),
                (taps_hbm, taps_ref),
                (outer_hbm, outer_ref),
                (inner_hbm, inner_ref),
                (inner_t_hbm, inner_t_ref),
                (outer_t_hbm, outer_t_ref),
                (q_hbm, q_ref),
                (stream_hbm, stream_ref),
            ]
        )
    ]
    for load in loads:
        load.start()

    def block_at(zz, xx, cc):
        return (zz * 2 + xx) * 2 + cc

    piece = weights.shape[1] // PIECES

    def weight_copy(block, part, target, way):
        held = weights.at[block, pl.ds(part * piece, piece)]
        return pltpu.make_async_remote_copy(
            src_ref=held,
            dst_ref=held,
            send_sem=send_weight.at[block * PIECES + part, way],
            recv_sem=recv_weight.at[block * PIECES + part],
            device_id={"seq": target},
            device_id_type=mesh_ids,
        )

    to_core = block_at(layer, side, 1 - core)
    to_side = block_at(layer, 1 - side, core)

    def act(copy, sending):
        if sending:
            copy.start()
        else:
            copy.wait_send()

    def spread(block, part, sending, up, down):
        if up:

            @pl.when(layer + 1 < depth)
            def _():
                act(weight_copy(block, part, me + 4, 2), sending)

        if down:

            @pl.when(layer > 0)
            def _():
                act(weight_copy(block, part, me - 4, 3), sending)

        act(weight_copy(block, part, to_side, 1), sending)
        act(weight_copy(block, part, to_core, 0), sending)

    def arrive(block, part):
        weight_copy(block, part, to_core, 0).wait_recv()

    def at_distance(d, body):
        for sign in (-1, 1) if d else (1,):
            zz = layer + sign * d

            @pl.when((zz >= 0) & (zz < depth))
            def _():
                body(zz, sign)

    def from_layer(d, *parts):
        if d >= depth:
            return

        def body(zz, sign, part):
            block = block_at(zz, side, core)
            arrive(block, part)
            spread(block, part, True, sign < 0, sign > 0)

        for part in parts or range(PIECES):
            at_distance(d, functools.partial(body, part=part))

    def from_side(d, *parts):
        if d >= depth:
            return

        def body(zz, sign, part):
            block = block_at(zz, 1 - side, core)
            arrive(block, part)
            weight_copy(block, part, to_core, 0).start()

        for part in parts or range(PIECES):
            at_distance(d, functools.partial(body, part=part))

    def share_copy(b):
        return pltpu.make_async_remote_copy(
            src_ref=shares.at[b],
            dst_ref=arrived.at[b],
            send_sem=send_share.at[b],
            recv_sem=recv_share.at[b],
            device_id={"tp": 1 - tp},
            device_id_type=mesh_ids,
        )

    def project(d):
        def body(zz, sign):
            for xx in (0, 1):
                for part in range(PIECES):
                    arrive(block_at(zz, xx, 1 - core), part)

            def step(i, carry):
                block = zz * 4 + i
                terms = jnp.dot(gated[...], weights[block], preferred_element_type=jnp.float32)
                b = block % half

                @pl.when(block // half == tp)
                def _():
                    kept[b] = terms

                @pl.when(block // half != tp)
                def _():
                    shares[b] = terms.astype(jnp.bfloat16)
                    share_copy(b).start()

                return carry

            lax.fori_loop(0, 4, step, 0)

        if d < depth:
            at_distance(d, body)

    barrier = pltpu.get_barrier_semaphore()
    for i in range(1, peers):
        pl.semaphore_signal(
            barrier,
            inc=1,
            device_id={"seq": lax.rem(me + i, peers)},
            device_id_type=mesh_ids,
        )
    pl.semaphore_signal(barrier, inc=1, device_id={"tp": 1 - tp}, device_id_type=mesh_ids)

    def mix(p, carry):
        cols = pl.ds(pl.multiple_of(p * LANES, LANES), LANES)
        product = k_ref[:, cols].astype(jnp.float32) * v_ref[:, cols].astype(jnp.float32)
        sent[p] = product.astype(jnp.bfloat16).reshape(per, LANES, LANES)
        return carry

    lax.fori_loop(0, peers, mix, 0)
    pl.semaphore_wait(barrier, peers)

    first_copies = []
    for i in range(1, peers):
        target = lax.rem(me + i, peers)
        copy = pltpu.make_async_remote_copy(
            src_ref=sent.at[target],
            dst_ref=signal.at[pl.ds(me * per, per)],
            send_sem=send_one.at[i],
            recv_sem=recv_one.at[i],
            device_id={"seq": target},
            device_id_type=mesh_ids,
        )
        copy.start()
        first_copies.append(copy)
    signal[pl.ds(me * per, per)] = sent[me]
    loads[0].wait()
    for part in range(PIECES):
        spread(me, part, True, True, True)

    def outer_stage(source):
        def step(g, carry):
            lo = pl.ds(pl.multiple_of(g * 2 * GROUP, 2 * GROUP), GROUP)
            hi = pl.ds(pl.multiple_of(g * 2 * GROUP + GROUP, GROUP), GROUP)
            block = jnp.concatenate(
                [
                    source[:, lo, :].reshape(slots * GROUP, LANES),
                    source[:, hi, :].reshape(slots * GROUP, LANES),
                ],
                axis=1,
            )
            y = jnp.dot(outer_ref[...], block, preferred_element_type=jnp.float32)
            y = y.astype(jnp.bfloat16)
            work[:, :, lo, :] = y[:, :LANES].reshape(slots, 2, GROUP, LANES)
            work[:, :, hi, :] = y[:, LANES:].reshape(slots, 2, GROUP, LANES)
            return carry

        lax.fori_loop(0, LANES // (2 * GROUP), step, 0)

    def inner_forward(s):
        return jnp.dot(
            inner_ref[s],
            work[s].reshape(2 * LANES, LANES),
            preferred_element_type=jnp.float32,
        )

    def turn(n, carry):
        cols = pl.ds(pl.multiple_of(n * LANES, LANES), LANES)
        turned[n] = taps_ref[:, cols].T.astype(jnp.bfloat16)
        return carry

    loads[1].wait()
    lax.fori_loop(0, slots, turn, 0)
    loads[2].wait()
    outer_stage(turned)
    loads[3].wait()
    from_layer(1, 0)

    def tap_step(s, carry):
        spectrum[s] = inner_forward(s)
        return carry

    lax.fori_loop(0, slots, tap_step, 0, unroll=2)
    from_layer(1, 1)

    for copy in first_copies:
        copy.wait_recv()
    outer_stage(signal)
    from_layer(1, 2, 3)
    loads[4].wait()

    def middle(s, slot_zero):
        p = spectral_product(inner_forward(s), spectrum[s], slot_zero)
        q = jnp.dot(inner_t_ref[s], p.astype(jnp.bfloat16), preferred_element_type=jnp.float32)
        work[s] = q.astype(jnp.bfloat16).reshape(2, LANES, LANES)

    middle(0, True)

    def middle_step(s, carry):
        middle(s, False)
        return carry

    lax.fori_loop(1, slots // 2, middle_step, 0, unroll=2)
    from_layer(2, 0)
    lax.fori_loop(slots // 2, slots, middle_step, 0, unroll=2)
    from_layer(2, 1)

    loads[5].wait()

    def outer_back(g, carry):
        lo = pl.ds(pl.multiple_of(g * 2 * GROUP, 2 * GROUP), GROUP)
        hi = pl.ds(pl.multiple_of(g * 2 * GROUP + GROUP, GROUP), GROUP)
        block = jnp.concatenate(
            [
                work[:, :, lo, :].reshape(2 * slots * GROUP, LANES),
                work[:, :, hi, :].reshape(2 * slots * GROUP, LANES),
            ],
            axis=1,
        )
        y = jnp.dot(outer_t_ref[...], block, preferred_element_type=jnp.float32)
        y = (y * (2.0 / total)).astype(jnp.bfloat16)
        result[:, lo, :] = y[:, :LANES].reshape(slots, GROUP, LANES)
        result[:, hi, :] = y[:, LANES:].reshape(slots, GROUP, LANES)
        return carry

    lax.fori_loop(0, LANES // (2 * GROUP), outer_back, 0)

    second_copies = []
    for i in range(1, peers):
        target = lax.rem(me + i, peers)
        copy = pltpu.make_async_remote_copy(
            src_ref=result.at[pl.ds(target * per, per)],
            dst_ref=returned.at[me],
            send_sem=send_two.at[i],
            recv_sem=recv_two.at[i],
            device_id={"seq": target},
            device_id_type=mesh_ids,
        )
        copy.start()
        second_copies.append(copy)
    from_side(0)
    from_layer(2, 2, 3)
    from_side(1)
    from_layer(3, 0, 1)
    loads[6].wait()

    def gate(p, block):
        cols = pl.ds(pl.multiple_of(p * LANES, LANES), LANES)
        conv = block.reshape(rows, LANES).astype(jnp.float32)
        gated[:, cols] = (q_ref[:, cols].astype(jnp.float32) * conv).astype(jnp.bfloat16)

    gate(me, result[pl.ds(me * per, per)])
    for i, copy in enumerate(second_copies, 1):
        copy.wait_recv()
        source = lax.rem(me + peers - i, peers)
        gate(source, returned[source])
    from_layer(3, 2, 3)
    project(0)
    from_side(2)
    project(1)
    project(2)
    for d in range(3, depth):
        if d > 3:
            from_layer(d)
        from_side(d)
        project(d)

    loads[7].wait()
    width = kept.shape[2]

    def finish(b, carry):
        share_copy(b).wait_recv()
        cols = pl.ds(pl.multiple_of(b * width, width), width)
        added = kept[b] + arrived[b].astype(jnp.float32)
        out_ref[:, cols] = (stream_ref[:, cols].astype(jnp.float32) + added).astype(jnp.bfloat16)
        return carry

    lax.fori_loop(0, half, finish, 0)

    for copy in first_copies + second_copies:
        copy.wait_send()
    for part in range(PIECES):
        spread(me, part, False, True, True)
    for d in range(depth):

        def settle(zz, sign):
            for part in range(PIECES):
                if d:
                    spread(block_at(zz, side, core), part, False, sign < 0, sign > 0)
                weight_copy(block_at(zz, 1 - side, core), part, to_core, 0).wait_send()

        at_distance(d, settle)

    def sent_share(b, carry):
        share_copy(b).wait_send()
        return carry

    lax.fori_loop(0, half, sent_share, 0)


def fused_mixer(q_feat, k_feat, v_feat, stream, filters, w_out, peers):
    rows, columns = q_feat.shape
    chans, length = filters.shape
    slots = length // LANES
    per = rows // LANES
    tables = spectral_tables(length)
    vmem = pl.BlockSpec(memory_space=pltpu.VMEM)
    anywhere = pl.BlockSpec(memory_space=pl.ANY)
    bf16 = jnp.bfloat16
    depth, width = w_out.shape
    half = peers // 2
    dma = pltpu.SemaphoreType.DMA
    return pl.pallas_call(
        functools.partial(mixer_kernel, peers),
        out_shape=jax.ShapeDtypeStruct((rows, columns), bf16),
        in_specs=[vmem] * 2 + [anywhere] * 8,
        out_specs=vmem,
        scratch_shapes=[
            pltpu.VMEM((rows, columns), bf16),
            pltpu.VMEM((rows, columns), bf16),
            pltpu.VMEM((chans, length), jnp.float32),
        ]
        + [pltpu.VMEM(t.shape, bf16) for t in tables]
        + [
            pltpu.VMEM((peers, per, LANES, LANES), bf16),
            pltpu.VMEM((slots, LANES, LANES), bf16),
            pltpu.VMEM((slots, LANES, LANES), bf16),
            pltpu.VMEM((peers, per, LANES, LANES), bf16),
            pltpu.VMEM((slots, LANES, LANES), bf16),
            pltpu.VMEM((slots, 2 * LANES, LANES), jnp.float32),
            pltpu.VMEM((slots, 2, LANES, LANES), bf16),
            pltpu.VMEM((rows, columns), bf16),
            pltpu.VMEM((peers, depth, width), bf16),
            pltpu.VMEM((half, rows, width), jnp.float32),
            pltpu.VMEM((half, rows, width), bf16),
            pltpu.VMEM((half, rows, width), bf16),
            dma((8,)),
            dma((peers,)),
            dma((peers,)),
            dma((peers,)),
            dma((peers,)),
            dma((peers * PIECES, 4)),
            dma((peers * PIECES,)),
            dma((half,)),
            dma((half,)),
        ],
        compiler_params=pltpu.CompilerParams(
            collective_id=0, has_side_effects=True, vmem_limit_bytes=58 * 1024 * 1024
        ),
        cost_estimate=pl.CostEstimate(
            flops=2 * rows * depth * width * peers,
            bytes_accessed=16 * 1024 * 1024,
            transcendentals=0,
        ),
    )(k_feat, v_feat, q_feat, stream, filters, w_out, *[jnp.asarray(t) for t in tables])


def gated_features(q_feat, k_feat, v_feat, filters):
    mixed = (k_feat.astype(jnp.float32) * v_feat.astype(jnp.float32)).astype(jnp.bfloat16)
    sent_mixed = lax.all_to_all(mixed.T, "seq", split_axis=0, concat_axis=1, tiled=True)
    conv_out = long_conv(sent_mixed, filters).astype(jnp.bfloat16)
    returned_output = lax.all_to_all(conv_out, "seq", split_axis=1, concat_axis=0, tiled=True)
    return (q_feat.astype(jnp.float32) * returned_output.T.astype(jnp.float32)).astype(
        jnp.bfloat16
    )


def local(q_feat, k_feat, v_feat, stream, filters, w_out):
    peers = lax.axis_size("seq")
    if (
        filters.shape[0] == LANES
        and q_feat.shape[0] % LANES == 0
        and peers % 4 == 0
        and lax.axis_size("tp") == 2
        and w_out.shape[1] % LANES == 0
    ):
        return fused_mixer(q_feat, k_feat, v_feat, stream, filters, w_out, peers)
    gated = gated_features(q_feat, k_feat, v_feat, filters)
    terms = jnp.dot(
        gated, lax.all_gather(w_out, "seq", axis=1, tiled=True), preferred_element_type=jnp.float32
    )
    accumulated_total = lax.psum_scatter(
        terms.astype(jnp.bfloat16), "tp", scatter_dimension=1, tiled=True
    ).astype(jnp.float32)
    return (stream.astype(jnp.float32) + accumulated_total).astype(jnp.bfloat16)


def solution(mesh):
    return jax.shard_map(
        local,
        mesh=mesh,
        in_specs=(
            P("seq", "tp"),
            P("seq", "tp"),
            P("seq", "tp"),
            P("seq", "tp"),
            P(("tp", "seq"), None),
            P("tp", "seq"),
        ),
        out_specs=P("seq", "tp"),
        check_vma=False,
    )
```

```python
import functools
import math

import jax
import jax.numpy as jnp
import numpy as np
from jax import lax
from jax.experimental import pallas as pl
from jax.experimental.pallas import tpu as pltpu
from jax.sharding import PartitionSpec as P

LANES = 128
GROUP = 16
PIECES = 4

def window_extent(total):
    chosen = 2
    for normalizing_multiplier in range(2, math.isqrt(total) + 1, 2):
        if total % normalizing_multiplier == 0:
            chosen = normalizing_multiplier
    return chosen


def make_tables(first, second, total):
    rows = jnp.arange(first, dtype=jnp.int32)
    half_rows = jnp.arange(first // 2, dtype=jnp.int32)
    columns = jnp.arange(second, dtype=jnp.int32)
    angle_one = (
        2.0 * math.pi / first * (rows[:, None] * half_rows[None, :] % first).astype(jnp.float32)
    )
    angle_two = (
        2.0 * math.pi / second * (columns[:, None] * columns[None, :] % second).astype(jnp.float32)
    )
    angle_twist = (
        2.0 * math.pi / total * (rows[:, None] * columns[None, :] % total).astype(jnp.float32)
    )
    return (
        jnp.cos(angle_one),
        jnp.sin(angle_one),
        jnp.cos(angle_two),
        jnp.sin(angle_two),
        jnp.cos(angle_twist),
        jnp.sin(angle_twist),
    )


def forward_transform(signal, tables, first, second):
    cosine_first, sin_one, cos_two, sin_two, cos_twist, sin_twist = tables
    chans = signal.shape[0]
    shaped = signal.reshape(chans, first // 2, second)
    highest = lax.Precision.HIGHEST
    real_a = jnp.einsum("kn,cnm->ckm", cosine_first, shaped, precision=highest)
    imaginary_left = -jnp.einsum("kn,cnm->ckm", sin_one, shaped, precision=highest)
    real_b = real_a * cos_twist + imaginary_left * sin_twist
    imag_b = imaginary_left * cos_twist - real_a * sin_twist
    real_x = jnp.einsum("ckn,nm->ckm", real_b, cos_two, precision=highest) + jnp.einsum(
        "ckn,nm->ckm", imag_b, sin_two, precision=highest
    )
    imag_x = jnp.einsum("ckn,nm->ckm", imag_b, cos_two, precision=highest) - jnp.einsum(
        "ckn,nm->ckm", real_b, sin_two, precision=highest
    )
    return (real_x, imag_x)


def inverse_transform(real_p, imag_p, tables, first, second):
    cosine_first, sin_one, cos_two, sin_two, cos_twist, sin_twist = tables
    highest = lax.Precision.HIGHEST
    real_d = jnp.einsum("ckn,nm->ckm", real_p, cos_two, precision=highest) - jnp.einsum(
        "ckn,nm->ckm", imag_p, sin_two, precision=highest
    )
    imag_d = jnp.einsum("ckn,nm->ckm", real_p, sin_two, precision=highest) + jnp.einsum(
        "ckn,nm->ckm", imag_p, cos_two, precision=highest
    )
    kernel_spectrum_real = real_d * cos_twist - imag_d * sin_twist
    imag_e = real_d * sin_twist + imag_d * cos_twist
    result = jnp.einsum(
        "kn,ckm->cnm", cosine_first, kernel_spectrum_real, precision=highest
    ) - jnp.einsum("kn,ckm->cnm", sin_one, imag_e, precision=highest)
    return result / (first * second)


def long_conv(mixed_cols, filters):
    chans, length = filters.shape
    total = 2 * length
    first = window_extent(total)
    second = total // first
    tables = make_tables(first, second, total)
    stacked = jnp.concatenate([mixed_cols.astype(jnp.float32), filters], axis=0)
    real_x, imag_x = forward_transform(stacked, tables, first, second)
    real_p = real_x[:chans] * real_x[chans:] - imag_x[:chans] * imag_x[chans:]
    imag_p = real_x[:chans] * imag_x[chans:] + imag_x[:chans] * real_x[chans:]
    result = inverse_transform(real_p, imag_p, tables, first, second)
    return result.reshape(chans, length)


def spectral_tables(length):
    total = 2 * length
    first = total // LANES
    slots = first // 2
    n_one = np.arange(slots)
    base = np.zeros((slots, 2, slots))
    for s in range(1, slots):
        angle = 2.0 * np.pi * (s * n_one % first) / first
        base[s, 0] = np.cos(angle)
        base[s, 1] = -np.sin(angle)
    base[0, 0] = 1.0
    base[0, 1] = 1.0 - 2.0 * (n_one % 2)
    outer = np.kron(base.reshape(first, slots), np.eye(GROUP))
    n_two = np.arange(LANES)
    k_two = np.arange(LANES)
    inner = np.zeros((slots, 2 * LANES, 2 * LANES))

    def wave(k_one, rows):
        turns = (first * rows[:, None] + k_one) * n_two[None, :] % total
        return np.exp(-2j * np.pi * turns / total)

    for s in range(1, slots):
        t = wave(s, k_two)
        inner[s] = np.block([[t.real, -t.imag], [t.imag, t.real]])
    half = LANES // 2
    zero = wave(0, k_two[:half])
    mid = wave(slots, k_two[:half])
    inner[0, :half, :LANES] = zero.real
    inner[0, half:LANES, LANES:] = mid.real
    inner[0, LANES : LANES + half, :LANES] = zero.imag
    inner[0, LANES + half :, LANES:] = mid.imag
    inner[0, LANES, :LANES] = 1.0 - 2.0 * (n_two % 2)
    cast = lambda a: np.ascontiguousarray(a).astype(jnp.bfloat16)
    return cast(outer), cast(outer.T), cast(inner), cast(inner.transpose(0, 2, 1))


def spectral_product(a, b, slot_zero):
    a_re, a_im = a[:LANES], a[LANES:]
    b_re, b_im = b[:LANES], b[LANES:]
    rr, ii = a_re * b_re, a_im * b_im
    p_re = rr - ii
    p_im = a_re * b_im + a_im * b_re
    if slot_zero:
        top = lax.broadcasted_iota(jnp.int32, p_re.shape, 0) == 0
        p_re = jnp.where(top, 0.5 * rr, p_re)
        p_im = jnp.where(top, 0.5 * ii, p_im)
    return jnp.concatenate([p_re, p_im], axis=0)


def mixer_kernel(
    peers,
    k_ref,
    v_ref,
    q_hbm,
    stream_hbm,
    taps_hbm,
    weights_hbm,
    outer_hbm,
    outer_t_hbm,
    inner_hbm,
    inner_t_hbm,
    out_ref,
    q_ref,
    stream_ref,
    taps_ref,
    outer_ref,
    outer_t_ref,
    inner_ref,
    inner_t_ref,
    sent,
    signal,
    result,
    returned,
    turned,
    spectrum,
    work,
    gated,
    weights,
    kept,
    shares,
    arrived,
    passed,
    handed,
    load_sem,
    send_one,
    recv_one,
    send_two,
    recv_two,
    send_weight,
    recv_weight,
    send_share,
    recv_share,
    send_gated,
    recv_gated,
    send_passed,
    recv_passed,
):
    me = lax.axis_index("seq")
    tp = lax.axis_index("tp")
    rows = k_ref.shape[0]
    slots = signal.shape[0]
    per = slots // peers
    total = 2 * slots * LANES
    mesh_ids = pl.DeviceIdType.MESH
    depth = peers // 4
    width = weights.shape[2]
    layer, side, core = me // 4, (me // 2) % 2, me % 2

    loads = [
        pltpu.make_async_copy(source, target, load_sem.at[i])
        for i, (source, target) in enumerate(
            [
                (weights_hbm, weights.at[layer * 2 + core]),
                (taps_hbm, taps_ref),
                (outer_hbm, outer_ref),
                (inner_hbm, inner_ref),
                (inner_t_hbm, inner_t_ref),
                (outer_t_hbm, outer_t_ref),
                (q_hbm, q_ref),
                (stream_hbm, stream_ref),
            ]
        )
    ]
    for load in loads:
        load.start()

    piece = weights.shape[1] // PIECES

    def weight_copy(block, part, target, way):
        held = weights.at[block, pl.ds(part * piece, piece)]
        return pltpu.make_async_remote_copy(
            src_ref=held,
            dst_ref=held,
            send_sem=send_weight.at[block * PIECES + part, way],
            recv_sem=recv_weight.at[block * PIECES + part],
            device_id={"seq": target},
            device_id_type=mesh_ids,
        )

    to_core = (layer * 2 + side) * 2 + 1 - core
    to_side = (layer * 2 + 1 - side) * 2 + core
    mine = layer * 2 + core

    def act(copy, sending):
        if sending:
            copy.start()
        else:
            copy.wait_send()

    def spread(block, part, sending, up, down):
        if up:

            @pl.when(layer + 1 < depth)
            def _():
                act(weight_copy(block, part, me + 4, 1), sending)

        if down:

            @pl.when(layer > 0)
            def _():
                act(weight_copy(block, part, me - 4, 2), sending)

        act(weight_copy(block, part, to_core, 0), sending)

    def arrive(block, part):
        weight_copy(block, part, to_core, 0).wait_recv()

    def at_distance(d, body):
        for sign in (-1, 1) if d else (1,):
            zz = layer + sign * d

            @pl.when((zz >= 0) & (zz < depth))
            def _():
                body(zz, sign)

    def from_layer(d, *parts):
        if d >= depth:
            return

        def body(zz, sign, part):
            block = zz * 2 + core
            arrive(block, part)
            spread(block, part, True, sign < 0, sign > 0)

        for part in parts or range(PIECES):
            at_distance(d, functools.partial(body, part=part))

    def share_copy(b):
        return pltpu.make_async_remote_copy(
            src_ref=shares.at[b],
            dst_ref=arrived.at[b],
            send_sem=send_share.at[b],
            recv_sem=recv_share.at[b],
            device_id={"tp": 1 - tp},
            device_id_type=mesh_ids,
        )

    def gated_copy(p):
        cols = pl.ds(pl.multiple_of(p * LANES, LANES), LANES)
        return pltpu.make_async_remote_copy(
            src_ref=gated.at[0, :, cols],
            dst_ref=gated.at[1, :, cols],
            send_sem=send_gated.at[p],
            recv_sem=recv_gated.at[p],
            device_id={"seq": to_side},
            device_id_type=mesh_ids,
        )

    def passed_copy(b):
        return pltpu.make_async_remote_copy(
            src_ref=passed.at[b],
            dst_ref=handed.at[b],
            send_sem=send_passed.at[b],
            recv_sem=recv_passed.at[b],
            device_id={"seq": to_side},
            device_id_type=mesh_ids,
        )

    def project(d):
        def body(zz, sign):
            for part in range(PIECES):
                arrive(zz * 2 + 1 - core, part)

            def step(i, carry):
                block = zz * 2 + i
                terms = jnp.dot(
                    gated[...].reshape(2 * rows, gated.shape[2]),
                    weights[block],
                    preferred_element_type=jnp.float32,
                )
                b = block % depth

                @pl.when(block // depth == tp)
                def _():
                    kept[b] = terms

                @pl.when(block // depth != tp)
                def _():
                    shares[b] = terms.astype(jnp.bfloat16)
                    share_copy(b).start()

                return carry

            lax.fori_loop(0, 2, step, 0)

        if d < depth:
            at_distance(d, body)

    def place(b, xx, values):
        spot = (b // 2) * 4 + xx * 2 + b % 2
        cols = pl.ds(pl.multiple_of(spot * width, width), width)
        out_ref[:, cols] = (stream_ref[:, cols].astype(jnp.float32) + values).astype(jnp.bfloat16)

    def finish(d):
        def body(zz, sign):
            @pl.when(zz * 2 // depth == tp)
            def _():
                for i in (0, 1):
                    b = zz * 2 + i - tp * depth
                    share_copy(b).wait_recv()
                    passed[b] = (
                        kept[b, rows:, :] + arrived[b, rows:, :].astype(jnp.float32)
                    ).astype(jnp.bfloat16)
                    passed_copy(b).start()
                    place(b, side, kept[b, :rows, :] + arrived[b, :rows, :].astype(jnp.float32))

        if d < depth:
            at_distance(d, body)

    barrier = pltpu.get_barrier_semaphore()
    for i in range(1, peers):
        pl.semaphore_signal(
            barrier,
            inc=1,
            device_id={"seq": lax.rem(me + i, peers)},
            device_id_type=mesh_ids,
        )
    pl.semaphore_signal(barrier, inc=1, device_id={"tp": 1 - tp}, device_id_type=mesh_ids)

    def mix(p, carry):
        cols = pl.ds(pl.multiple_of(p * LANES, LANES), LANES)
        product = k_ref[:, cols].astype(jnp.float32) * v_ref[:, cols].astype(jnp.float32)
        sent[p] = product.astype(jnp.bfloat16).reshape(per, LANES, LANES)
        return carry

    lax.fori_loop(0, peers, mix, 0)
    pl.semaphore_wait(barrier, peers)

    first_copies = []
    for i in range(1, peers):
        target = lax.rem(me + i, peers)
        copy = pltpu.make_async_remote_copy(
            src_ref=sent.at[target],
            dst_ref=signal.at[pl.ds(me * per, per)],
            send_sem=send_one.at[i],
            recv_sem=recv_one.at[i],
            device_id={"seq": target},
            device_id_type=mesh_ids,
        )
        copy.start()
        first_copies.append(copy)
    signal[pl.ds(me * per, per)] = sent[me]
    loads[0].wait()
    for part in range(PIECES):
        spread(mine, part, True, True, True)

    def outer_stage(source):
        def step(g, carry):
            lo = pl.ds(pl.multiple_of(g * 2 * GROUP, 2 * GROUP), GROUP)
            hi = pl.ds(pl.multiple_of(g * 2 * GROUP + GROUP, GROUP), GROUP)
            block = jnp.concatenate(
                [
                    source[:, lo, :].reshape(slots * GROUP, LANES),
                    source[:, hi, :].reshape(slots * GROUP, LANES),
                ],
                axis=1,
            )
            y = jnp.dot(outer_ref[...], block, preferred_element_type=jnp.float32)
            y = y.astype(jnp.bfloat16)
            work[:, :, lo, :] = y[:, :LANES].reshape(slots, 2, GROUP, LANES)
            work[:, :, hi, :] = y[:, LANES:].reshape(slots, 2, GROUP, LANES)
            return carry

        lax.fori_loop(0, LANES // (2 * GROUP), step, 0)

    def inner_forward(s):
        return jnp.dot(
            inner_ref[s],
            work[s].reshape(2 * LANES, LANES),
            preferred_element_type=jnp.float32,
        )

    def turn(n, carry):
        cols = pl.ds(pl.multiple_of(n * LANES, LANES), LANES)
        turned[n] = taps_ref[:, cols].T.astype(jnp.bfloat16)
        return carry

    loads[1].wait()
    lax.fori_loop(0, slots, turn, 0)
    loads[2].wait()
    outer_stage(turned)
    loads[3].wait()
    from_layer(1, 0)

    def tap_step(s, carry):
        spectrum[s] = inner_forward(s)
        return carry

    lax.fori_loop(0, slots, tap_step, 0, unroll=2)
    from_layer(1, 1)

    for copy in first_copies:
        copy.wait_recv()
    outer_stage(signal)
    from_layer(1, 2, 3)
    loads[4].wait()

    def middle(s, slot_zero):
        p = spectral_product(inner_forward(s), spectrum[s], slot_zero)
        q = jnp.dot(inner_t_ref[s], p.astype(jnp.bfloat16), preferred_element_type=jnp.float32)
        work[s] = q.astype(jnp.bfloat16).reshape(2, LANES, LANES)

    middle(0, True)

    def middle_step(s, carry):
        middle(s, False)
        return carry

    lax.fori_loop(1, slots // 2, middle_step, 0, unroll=2)
    from_layer(2, 0)
    lax.fori_loop(slots // 2, slots, middle_step, 0, unroll=2)
    from_layer(2, 1)

    loads[5].wait()

    def outer_back(g, carry):
        lo = pl.ds(pl.multiple_of(g * 2 * GROUP, 2 * GROUP), GROUP)
        hi = pl.ds(pl.multiple_of(g * 2 * GROUP + GROUP, GROUP), GROUP)
        block = jnp.concatenate(
            [
                work[:, :, lo, :].reshape(2 * slots * GROUP, LANES),
                work[:, :, hi, :].reshape(2 * slots * GROUP, LANES),
            ],
            axis=1,
        )
        y = jnp.dot(outer_t_ref[...], block, preferred_element_type=jnp.float32)
        y = (y * (2.0 / total)).astype(jnp.bfloat16)
        result[:, lo, :] = y[:, :LANES].reshape(slots, GROUP, LANES)
        result[:, hi, :] = y[:, LANES:].reshape(slots, GROUP, LANES)
        return carry

    lax.fori_loop(0, LANES // (2 * GROUP), outer_back, 0)

    second_copies = []
    for i in range(1, peers):
        target = lax.rem(me + i, peers)
        copy = pltpu.make_async_remote_copy(
            src_ref=result.at[pl.ds(target * per, per)],
            dst_ref=returned.at[me],
            send_sem=send_two.at[i],
            recv_sem=recv_two.at[i],
            device_id={"seq": target},
            device_id_type=mesh_ids,
        )
        copy.start()
        second_copies.append(copy)
    from_layer(2, 2, 3)
    loads[6].wait()

    def gate(p, block):
        cols = pl.ds(pl.multiple_of(p * LANES, LANES), LANES)
        conv = block.reshape(rows, LANES).astype(jnp.float32)
        gated[0, :, cols] = (q_ref[:, cols].astype(jnp.float32) * conv).astype(jnp.bfloat16)
        gated_copy(p).start()

    gate(me, result[pl.ds(me * per, per)])
    for i, copy in enumerate(second_copies, 1):
        copy.wait_recv()
        source = lax.rem(me + peers - i, peers)
        gate(source, returned[source])
    loads[7].wait()
    from_layer(3, 0, 1)

    def gated_in(p, carry):
        gated_copy(p).wait_recv()
        return carry

    lax.fori_loop(0, peers, gated_in, 0)
    project(0)
    project(1)
    finish(0)
    project(2)
    finish(1)
    from_layer(3, 2, 3)
    project(3)
    finish(2)
    for d in range(4, depth):
        from_layer(d)
        project(d)
        finish(d - 1)
    if depth > 3:
        finish(depth - 1)

    def place_handed(b, carry):
        passed_copy(b).wait_recv()
        place(b, 1 - side, handed[b].astype(jnp.float32))
        return carry

    lax.fori_loop(0, depth, place_handed, 0)

    for copy in first_copies + second_copies:
        copy.wait_send()
    for part in range(PIECES):
        spread(mine, part, False, True, True)
    for d in range(1, depth):

        def settle(zz, sign):
            for part in range(PIECES):
                spread(zz * 2 + core, part, False, sign < 0, sign > 0)

        at_distance(d, settle)

    def sent_gated(p, carry):
        gated_copy(p).wait_send()
        return carry

    lax.fori_loop(0, peers, sent_gated, 0)

    def sent_share(b, carry):
        share_copy(b).wait_send()
        passed_copy(b).wait_send()
        return carry

    lax.fori_loop(0, depth, sent_share, 0)


def fused_mixer(q_feat, k_feat, v_feat, stream, filters, w_out, peers):
    rows, columns = q_feat.shape
    chans, length = filters.shape
    slots = length // LANES
    per = rows // LANES
    tables = spectral_tables(length)
    vmem = pl.BlockSpec(memory_space=pltpu.VMEM)
    anywhere = pl.BlockSpec(memory_space=pl.ANY)
    bf16 = jnp.bfloat16
    inner, width = w_out.shape
    depth = peers // 4
    dma = pltpu.SemaphoreType.DMA
    return pl.pallas_call(
        functools.partial(mixer_kernel, peers),
        out_shape=jax.ShapeDtypeStruct((rows, columns), bf16),
        in_specs=[vmem] * 2 + [anywhere] * 8,
        out_specs=vmem,
        scratch_shapes=[
            pltpu.VMEM((rows, columns), bf16),
            pltpu.VMEM((rows, columns), bf16),
            pltpu.VMEM((chans, length), jnp.float32),
        ]
        + [pltpu.VMEM(t.shape, bf16) for t in tables]
        + [
            pltpu.VMEM((peers, per, LANES, LANES), bf16),
            pltpu.VMEM((slots, LANES, LANES), bf16),
            pltpu.VMEM((slots, LANES, LANES), bf16),
            pltpu.VMEM((peers, per, LANES, LANES), bf16),
            pltpu.VMEM((slots, LANES, LANES), bf16),
            pltpu.VMEM((slots, 2 * LANES, LANES), jnp.float32),
            pltpu.VMEM((slots, 2, LANES, LANES), bf16),
            pltpu.VMEM((2, rows, columns), bf16),
            pltpu.VMEM((2 * depth, inner, width), bf16),
            pltpu.VMEM((depth, 2 * rows, width), jnp.float32),
            pltpu.VMEM((depth, 2 * rows, width), bf16),
            pltpu.VMEM((depth, 2 * rows, width), bf16),
            pltpu.VMEM((depth, rows, width), bf16),
            pltpu.VMEM((depth, rows, width), bf16),
            dma((8,)),
            dma((peers,)),
            dma((peers,)),
            dma((peers,)),
            dma((peers,)),
            dma((2 * depth * PIECES, 3)),
            dma((2 * depth * PIECES,)),
            dma((depth,)),
            dma((depth,)),
            dma((peers,)),
            dma((peers,)),
            dma((depth,)),
            dma((depth,)),
        ],
        compiler_params=pltpu.CompilerParams(
            collective_id=0, has_side_effects=True, vmem_limit_bytes=58 * 1024 * 1024
        ),
        cost_estimate=pl.CostEstimate(
            flops=2 * rows * inner * width * peers,
            bytes_accessed=16 * 1024 * 1024,
            transcendentals=0,
        ),
    )(k_feat, v_feat, q_feat, stream, filters, w_out, *[jnp.asarray(t) for t in tables])


def gated_features(q_feat, k_feat, v_feat, filters):
    mixed = (k_feat.astype(jnp.float32) * v_feat.astype(jnp.float32)).astype(jnp.bfloat16)
    sent_mixed = lax.all_to_all(mixed.T, "seq", split_axis=0, concat_axis=1, tiled=True)
    conv_out = long_conv(sent_mixed, filters).astype(jnp.bfloat16)
    returned_output = lax.all_to_all(conv_out, "seq", split_axis=1, concat_axis=0, tiled=True)
    return (q_feat.astype(jnp.float32) * returned_output.T.astype(jnp.float32)).astype(
        jnp.bfloat16
    )


def local(q_feat, k_feat, v_feat, stream, filters, w_out):
    peers = lax.axis_size("seq")
    if (
        filters.shape[0] == LANES
        and q_feat.shape[0] % LANES == 0
        and peers % 8 == 0
        and lax.axis_size("tp") == 2
        and w_out.shape[1] % LANES == 0
    ):
        return fused_mixer(q_feat, k_feat, v_feat, stream, filters, w_out, peers)
    gated = gated_features(q_feat, k_feat, v_feat, filters)
    terms = jnp.dot(
        gated, lax.all_gather(w_out, "seq", axis=1, tiled=True), preferred_element_type=jnp.float32
    )
    accumulated_total = lax.psum_scatter(
        terms.astype(jnp.bfloat16), "tp", scatter_dimension=1, tiled=True
    ).astype(jnp.float32)
    return (stream.astype(jnp.float32) + accumulated_total).astype(jnp.bfloat16)


def solution(mesh):
    return jax.shard_map(
        local,
        mesh=mesh,
        in_specs=(
            P("seq", "tp"),
            P("seq", "tp"),
            P("seq", "tp"),
            P("seq", "tp"),
            P(("tp", "seq"), None),
            P("tp", "seq"),
        ),
        out_specs=P("seq", "tp"),
        check_vma=False,
    )
```

```python
import functools
import math

import jax
import jax.numpy as jnp
import numpy as np
from jax import lax
from jax.experimental import pallas as pl
from jax.experimental.pallas import tpu as pltpu
from jax.sharding import PartitionSpec as P

LANES = 128
GROUP = 16
PIECES = 4

def window_extent(total):
    chosen = 2
    for normalizing_multiplier in range(2, math.isqrt(total) + 1, 2):
        if total % normalizing_multiplier == 0:
            chosen = normalizing_multiplier
    return chosen


def make_tables(first, second, total):
    rows = jnp.arange(first, dtype=jnp.int32)
    half_rows = jnp.arange(first // 2, dtype=jnp.int32)
    columns = jnp.arange(second, dtype=jnp.int32)
    angle_one = (
        2.0 * math.pi / first * (rows[:, None] * half_rows[None, :] % first).astype(jnp.float32)
    )
    angle_two = (
        2.0 * math.pi / second * (columns[:, None] * columns[None, :] % second).astype(jnp.float32)
    )
    angle_twist = (
        2.0 * math.pi / total * (rows[:, None] * columns[None, :] % total).astype(jnp.float32)
    )
    return (
        jnp.cos(angle_one),
        jnp.sin(angle_one),
        jnp.cos(angle_two),
        jnp.sin(angle_two),
        jnp.cos(angle_twist),
        jnp.sin(angle_twist),
    )


def forward_transform(signal, tables, first, second):
    cosine_first, sin_one, cos_two, sin_two, cos_twist, sin_twist = tables
    chans = signal.shape[0]
    shaped = signal.reshape(chans, first // 2, second)
    highest = lax.Precision.HIGHEST
    real_a = jnp.einsum("kn,cnm->ckm", cosine_first, shaped, precision=highest)
    imaginary_left = -jnp.einsum("kn,cnm->ckm", sin_one, shaped, precision=highest)
    real_b = real_a * cos_twist + imaginary_left * sin_twist
    imag_b = imaginary_left * cos_twist - real_a * sin_twist
    real_x = jnp.einsum("ckn,nm->ckm", real_b, cos_two, precision=highest) + jnp.einsum(
        "ckn,nm->ckm", imag_b, sin_two, precision=highest
    )
    imag_x = jnp.einsum("ckn,nm->ckm", imag_b, cos_two, precision=highest) - jnp.einsum(
        "ckn,nm->ckm", real_b, sin_two, precision=highest
    )
    return (real_x, imag_x)


def inverse_transform(real_p, imag_p, tables, first, second):
    cosine_first, sin_one, cos_two, sin_two, cos_twist, sin_twist = tables
    highest = lax.Precision.HIGHEST
    real_d = jnp.einsum("ckn,nm->ckm", real_p, cos_two, precision=highest) - jnp.einsum(
        "ckn,nm->ckm", imag_p, sin_two, precision=highest
    )
    imag_d = jnp.einsum("ckn,nm->ckm", real_p, sin_two, precision=highest) + jnp.einsum(
        "ckn,nm->ckm", imag_p, cos_two, precision=highest
    )
    kernel_spectrum_real = real_d * cos_twist - imag_d * sin_twist
    imag_e = real_d * sin_twist + imag_d * cos_twist
    result = jnp.einsum(
        "kn,ckm->cnm", cosine_first, kernel_spectrum_real, precision=highest
    ) - jnp.einsum("kn,ckm->cnm", sin_one, imag_e, precision=highest)
    return result / (first * second)


def long_conv(mixed_cols, filters):
    chans, length = filters.shape
    total = 2 * length
    first = window_extent(total)
    second = total // first
    tables = make_tables(first, second, total)
    stacked = jnp.concatenate([mixed_cols.astype(jnp.float32), filters], axis=0)
    real_x, imag_x = forward_transform(stacked, tables, first, second)
    real_p = real_x[:chans] * real_x[chans:] - imag_x[:chans] * imag_x[chans:]
    imag_p = real_x[:chans] * imag_x[chans:] + imag_x[:chans] * real_x[chans:]
    result = inverse_transform(real_p, imag_p, tables, first, second)
    return result.reshape(chans, length)


def spectral_tables(length):
    total = 2 * length
    first = total // LANES
    slots = first // 2
    n_one = np.arange(slots)
    base = np.zeros((slots, 2, slots))
    for s in range(1, slots):
        angle = 2.0 * np.pi * (s * n_one % first) / first
        base[s, 0] = np.cos(angle)
        base[s, 1] = -np.sin(angle)
    base[0, 0] = 1.0
    base[0, 1] = 1.0 - 2.0 * (n_one % 2)
    outer = np.kron(base.reshape(first, slots), np.eye(GROUP))
    n_two = np.arange(LANES)
    k_two = np.arange(LANES)
    inner = np.zeros((slots, 2 * LANES, 2 * LANES))

    def wave(k_one, rows):
        turns = (first * rows[:, None] + k_one) * n_two[None, :] % total
        return np.exp(-2j * np.pi * turns / total)

    for s in range(1, slots):
        t = wave(s, k_two)
        inner[s] = np.block([[t.real, -t.imag], [t.imag, t.real]])
    half = LANES // 2
    zero = wave(0, k_two[:half])
    mid = wave(slots, k_two[:half])
    inner[0, :half, :LANES] = zero.real
    inner[0, half:LANES, LANES:] = mid.real
    inner[0, LANES : LANES + half, :LANES] = zero.imag
    inner[0, LANES + half :, LANES:] = mid.imag
    inner[0, LANES, :LANES] = 1.0 - 2.0 * (n_two % 2)
    cast = lambda a: np.ascontiguousarray(a).astype(jnp.bfloat16)
    return cast(outer), cast(outer.T), cast(inner), cast(inner.transpose(0, 2, 1))


def spectral_product(a, b, slot_zero):
    a_re, a_im = a[:LANES], a[LANES:]
    b_re, b_im = b[:LANES], b[LANES:]
    rr, ii = a_re * b_re, a_im * b_im
    p_re = rr - ii
    p_im = a_re * b_im + a_im * b_re
    if slot_zero:
        top = lax.broadcasted_iota(jnp.int32, p_re.shape, 0) == 0
        p_re = jnp.where(top, 0.5 * rr, p_re)
        p_im = jnp.where(top, 0.5 * ii, p_im)
    return jnp.concatenate([p_re, p_im], axis=0)


def mixer_kernel(
    peers,
    k_ref,
    v_ref,
    q_hbm,
    stream_hbm,
    taps_hbm,
    weights_hbm,
    outer_hbm,
    outer_t_hbm,
    inner_hbm,
    inner_t_hbm,
    out_ref,
    q_ref,
    stream_ref,
    taps_ref,
    outer_ref,
    outer_t_ref,
    inner_ref,
    inner_t_ref,
    sent,
    signal,
    result,
    returned,
    turned,
    spectrum,
    work,
    gated,
    weights,
    kept,
    shares,
    arrived,
    load_sem,
    send_one,
    recv_one,
    send_two,
    recv_two,
    send_weight,
    recv_weight,
    send_share,
    recv_share,
):
    me = lax.axis_index("seq")
    tp = lax.axis_index("tp")
    rows = k_ref.shape[0]
    slots = signal.shape[0]
    per = slots // peers
    total = 2 * slots * LANES
    mesh_ids = pl.DeviceIdType.MESH
    depth = peers // 4
    half = peers // 2
    width = weights.shape[2]
    layer, side, core = me // 4, (me // 2) % 2, me % 2

    loads = [
        pltpu.make_async_copy(source, target, load_sem.at[i])
        for i, (source, target) in enumerate(
            [
                (weights_hbm, weights.at[me]),
                (taps_hbm, taps_ref),
                (outer_hbm, outer_ref),
                (inner_hbm, inner_ref),
                (inner_t_hbm, inner_t_ref),
                (outer_t_hbm, outer_t_ref),
                (q_hbm, q_ref),
                (stream_hbm, stream_ref),
            ]
        )
    ]
    for load in loads:
        load.start()

    def block_at(zz, xx, cc):
        return (zz * 2 + xx) * 2 + cc

    piece = weights.shape[1] // PIECES

    def weight_copy(block, part, target, way):
        held = weights.at[block, pl.ds(part * piece, piece)]
        return pltpu.make_async_remote_copy(
            src_ref=held,
            dst_ref=held,
            send_sem=send_weight.at[block * PIECES + part, way],
            recv_sem=recv_weight.at[block * PIECES + part],
            device_id={"seq": target},
            device_id_type=mesh_ids,
        )

    to_core = block_at(layer, side, 1 - core)
    to_side = block_at(layer, 1 - side, core)

    def act(copy, sending):
        if sending:
            copy.start()
        else:
            copy.wait_send()

    def spread(block, part, sending, up, down):
        if up:

            @pl.when(layer + 1 < depth)
            def _():
                act(weight_copy(block, part, me + 4, 2), sending)

        if down:

            @pl.when(layer > 0)
            def _():
                act(weight_copy(block, part, me - 4, 3), sending)

        act(weight_copy(block, part, to_side, 1), sending)
        act(weight_copy(block, part, to_core, 0), sending)

    def arrive(block, part):
        weight_copy(block, part, to_core, 0).wait_recv()

    def at_distance(d, body):
        for sign in (-1, 1) if d else (1,):
            zz = layer + sign * d

            @pl.when((zz >= 0) & (zz < depth))
            def _():
                body(zz, sign)

    def from_layer(d, *parts):
        if d >= depth:
            return

        def body(zz, sign, part):
            block = block_at(zz, side, core)
            arrive(block, part)
            spread(block, part, True, sign < 0, sign > 0)

        for part in parts or range(PIECES):
            at_distance(d, functools.partial(body, part=part))

    def from_side(d, *parts):
        if d >= depth:
            return

        def body(zz, sign, part):
            block = block_at(zz, 1 - side, core)
            arrive(block, part)
            weight_copy(block, part, to_core, 0).start()

        for part in parts or range(PIECES):
            at_distance(d, functools.partial(body, part=part))

    def share_copy(b):
        return pltpu.make_async_remote_copy(
            src_ref=shares.at[b],
            dst_ref=arrived.at[b],
            send_sem=send_share.at[b],
            recv_sem=recv_share.at[b],
            device_id={"tp": 1 - tp},
            device_id_type=mesh_ids,
        )

    def project(d, turns=(0, 1)):
        def body(zz, sign, turn):
            xx = side if turn == 0 else 1 - side
            for part in range(PIECES):
                arrive(block_at(zz, xx, 1 - core), part)

            def step(i, carry):
                block = block_at(zz, xx, i)
                terms = jnp.dot(gated[...], weights[block], preferred_element_type=jnp.float32)
                b = block % half

                @pl.when(block // half == tp)
                def _():
                    kept[b] = terms

                @pl.when(block // half != tp)
                def _():
                    shares[b] = terms.astype(jnp.bfloat16)
                    share_copy(b).start()

                return carry

            lax.fori_loop(0, 2, step, 0)

        if d < depth:
            for turn in turns:
                at_distance(d, functools.partial(body, turn=turn))

    def finish(d):
        def body(zz, sign):
            @pl.when(zz * 4 // half == tp)
            def _():
                def step(i, carry):
                    b = (zz * 4 + i) % half
                    share_copy(b).wait_recv()
                    cols = pl.ds(pl.multiple_of(b * width, width), width)
                    added = kept[b] + arrived[b].astype(jnp.float32)
                    total = stream_ref[:, cols].astype(jnp.float32) + added
                    out_ref[:, cols] = total.astype(jnp.bfloat16)
                    return carry

                lax.fori_loop(0, 4, step, 0)

        if d < depth:
            at_distance(d, body)

    barrier = pltpu.get_barrier_semaphore()
    for i in range(1, peers):
        pl.semaphore_signal(
            barrier,
            inc=1,
            device_id={"seq": lax.rem(me + i, peers)},
            device_id_type=mesh_ids,
        )
    pl.semaphore_signal(barrier, inc=1, device_id={"tp": 1 - tp}, device_id_type=mesh_ids)

    def mix(p, carry):
        cols = pl.ds(pl.multiple_of(p * LANES, LANES), LANES)
        product = k_ref[:, cols].astype(jnp.float32) * v_ref[:, cols].astype(jnp.float32)
        sent[p] = product.astype(jnp.bfloat16).reshape(per, LANES, LANES)
        return carry

    lax.fori_loop(0, peers, mix, 0)
    pl.semaphore_wait(barrier, peers)

    first_copies = []
    for i in range(1, peers):
        target = lax.rem(me + i, peers)
        copy = pltpu.make_async_remote_copy(
            src_ref=sent.at[target],
            dst_ref=signal.at[pl.ds(me * per, per)],
            send_sem=send_one.at[i],
            recv_sem=recv_one.at[i],
            device_id={"seq": target},
            device_id_type=mesh_ids,
        )
        copy.start()
        first_copies.append(copy)
    signal[pl.ds(me * per, per)] = sent[me]
    loads[0].wait()
    for part in range(PIECES // 2):
        spread(me, part, True, True, True)

    def outer_stage(source):
        def step(g, carry):
            lo = pl.ds(pl.multiple_of(g * 2 * GROUP, 2 * GROUP), GROUP)
            hi = pl.ds(pl.multiple_of(g * 2 * GROUP + GROUP, GROUP), GROUP)
            block = jnp.concatenate(
                [
                    source[:, lo, :].reshape(slots * GROUP, LANES),
                    source[:, hi, :].reshape(slots * GROUP, LANES),
                ],
                axis=1,
            )
            y = jnp.dot(outer_ref[...], block, preferred_element_type=jnp.float32)
            y = y.astype(jnp.bfloat16)
            work[:, :, lo, :] = y[:, :LANES].reshape(slots, 2, GROUP, LANES)
            work[:, :, hi, :] = y[:, LANES:].reshape(slots, 2, GROUP, LANES)
            return carry

        lax.fori_loop(0, LANES // (2 * GROUP), step, 0)

    def inner_forward(s):
        return jnp.dot(
            inner_ref[s],
            work[s].reshape(2 * LANES, LANES),
            preferred_element_type=jnp.float32,
        )

    def turn(n, carry):
        cols = pl.ds(pl.multiple_of(n * LANES, LANES), LANES)
        turned[n] = taps_ref[:, cols].T.astype(jnp.bfloat16)
        return carry

    loads[1].wait()
    lax.fori_loop(0, slots, turn, 0)
    loads[2].wait()
    outer_stage(turned)
    loads[3].wait()
    for part in range(PIECES // 2, PIECES):
        spread(me, part, True, True, True)

    def tap_step(s, carry):
        spectrum[s] = inner_forward(s)
        return carry

    lax.fori_loop(0, slots, tap_step, 0, unroll=4)
    from_layer(1, 0, 1)

    for copy in first_copies:
        copy.wait_recv()
    outer_stage(signal)
    from_layer(1, 2, 3)
    loads[4].wait()

    def middle(s, slot_zero):
        p = spectral_product(inner_forward(s), spectrum[s], slot_zero)
        q = jnp.dot(inner_t_ref[s], p.astype(jnp.bfloat16), preferred_element_type=jnp.float32)
        work[s] = q.astype(jnp.bfloat16).reshape(2, LANES, LANES)

    middle(0, True)

    def middle_step(s, carry):
        middle(s, False)
        return carry

    lax.fori_loop(1, slots // 2, middle_step, 0, unroll=4)
    from_layer(2, 0)
    lax.fori_loop(slots // 2, slots, middle_step, 0, unroll=4)
    from_layer(2, 1)

    loads[5].wait()

    def outer_back(g, carry):
        lo = pl.ds(pl.multiple_of(g * 2 * GROUP, 2 * GROUP), GROUP)
        hi = pl.ds(pl.multiple_of(g * 2 * GROUP + GROUP, GROUP), GROUP)
        block = jnp.concatenate(
            [
                work[:, :, lo, :].reshape(2 * slots * GROUP, LANES),
                work[:, :, hi, :].reshape(2 * slots * GROUP, LANES),
            ],
            axis=1,
        )
        y = jnp.dot(outer_t_ref[...], block, preferred_element_type=jnp.float32)
        y = (y * (2.0 / total)).astype(jnp.bfloat16)
        result[:, lo, :] = y[:, :LANES].reshape(slots, GROUP, LANES)
        result[:, hi, :] = y[:, LANES:].reshape(slots, GROUP, LANES)
        return carry

    lax.fori_loop(0, LANES // (2 * GROUP), outer_back, 0)

    second_copies = []
    for i in range(1, peers):
        target = lax.rem(me + i, peers)
        copy = pltpu.make_async_remote_copy(
            src_ref=result.at[pl.ds(target * per, per)],
            dst_ref=returned.at[me],
            send_sem=send_two.at[i],
            recv_sem=recv_two.at[i],
            device_id={"seq": target},
            device_id_type=mesh_ids,
        )
        copy.start()
        second_copies.append(copy)
    from_side(0)
    from_layer(2, 2, 3)
    from_side(1)
    from_layer(3)
    from_side(2)
    loads[6].wait()
    loads[7].wait()

    def gate(p, block):
        cols = pl.ds(pl.multiple_of(p * LANES, LANES), LANES)
        conv = block.reshape(rows, LANES).astype(jnp.float32)
        gated[:, cols] = (q_ref[:, cols].astype(jnp.float32) * conv).astype(jnp.bfloat16)

    gate(me, result[pl.ds(me * per, per)])
    for i, copy in enumerate(second_copies, 1):
        copy.wait_recv()
        source = lax.rem(me + peers - i, peers)
        gate(source, returned[source])
    project(0)
    project(1)
    finish(0)
    project(2)
    finish(1)
    project(3, (0,))
    from_side(3)
    project(3, (1,))
    finish(2)
    for d in range(4, depth):
        from_layer(d)
        from_side(d)
        project(d)
        finish(d - 1)
    if depth > 3:
        finish(depth - 1)

    for copy in first_copies + second_copies:
        copy.wait_send()
    for part in range(PIECES):
        spread(me, part, False, True, True)
    for d in range(depth):

        def settle(zz, sign):
            for part in range(PIECES):
                if d:
                    spread(block_at(zz, side, core), part, False, sign < 0, sign > 0)
                weight_copy(block_at(zz, 1 - side, core), part, to_core, 0).wait_send()

        at_distance(d, settle)

    def sent_share(b, carry):
        share_copy(b).wait_send()
        return carry

    lax.fori_loop(0, half, sent_share, 0)


def fused_mixer(q_feat, k_feat, v_feat, stream, filters, w_out, peers):
    rows, columns = q_feat.shape
    chans, length = filters.shape
    slots = length // LANES
    per = rows // LANES
    tables = spectral_tables(length)
    vmem = pl.BlockSpec(memory_space=pltpu.VMEM)
    anywhere = pl.BlockSpec(memory_space=pl.ANY)
    bf16 = jnp.bfloat16
    depth, width = w_out.shape
    half = peers // 2
    dma = pltpu.SemaphoreType.DMA
    return pl.pallas_call(
        functools.partial(mixer_kernel, peers),
        out_shape=jax.ShapeDtypeStruct((rows, columns), bf16),
        in_specs=[vmem] * 2 + [anywhere] * 8,
        out_specs=vmem,
        scratch_shapes=[
            pltpu.VMEM((rows, columns), bf16),
            pltpu.VMEM((rows, columns), bf16),
            pltpu.VMEM((chans, length), jnp.float32),
        ]
        + [pltpu.VMEM(t.shape, bf16) for t in tables]
        + [
            pltpu.VMEM((peers, per, LANES, LANES), bf16),
            pltpu.VMEM((slots, LANES, LANES), bf16),
            pltpu.VMEM((slots, LANES, LANES), bf16),
            pltpu.VMEM((peers, per, LANES, LANES), bf16),
            pltpu.VMEM((slots, LANES, LANES), bf16),
            pltpu.VMEM((slots, 2 * LANES, LANES), jnp.float32),
            pltpu.VMEM((slots, 2, LANES, LANES), bf16),
            pltpu.VMEM((rows, columns), bf16),
            pltpu.VMEM((peers, depth, width), bf16),
            pltpu.VMEM((half, rows, width), jnp.float32),
            pltpu.VMEM((half, rows, width), bf16),
            pltpu.VMEM((half, rows, width), bf16),
            dma((8,)),
            dma((peers,)),
            dma((peers,)),
            dma((peers,)),
            dma((peers,)),
            dma((peers * PIECES, 4)),
            dma((peers * PIECES,)),
            dma((half,)),
            dma((half,)),
        ],
        compiler_params=pltpu.CompilerParams(
            collective_id=0, has_side_effects=True, vmem_limit_bytes=58 * 1024 * 1024
        ),
        cost_estimate=pl.CostEstimate(
            flops=2 * rows * depth * width * peers,
            bytes_accessed=16 * 1024 * 1024,
            transcendentals=0,
        ),
    )(k_feat, v_feat, q_feat, stream, filters, w_out, *[jnp.asarray(t) for t in tables])


def gated_features(q_feat, k_feat, v_feat, filters):
    mixed = (k_feat.astype(jnp.float32) * v_feat.astype(jnp.float32)).astype(jnp.bfloat16)
    sent_mixed = lax.all_to_all(mixed.T, "seq", split_axis=0, concat_axis=1, tiled=True)
    conv_out = long_conv(sent_mixed, filters).astype(jnp.bfloat16)
    returned_output = lax.all_to_all(conv_out, "seq", split_axis=1, concat_axis=0, tiled=True)
    return (q_feat.astype(jnp.float32) * returned_output.T.astype(jnp.float32)).astype(
        jnp.bfloat16
    )


def local(q_feat, k_feat, v_feat, stream, filters, w_out):
    peers = lax.axis_size("seq")
    if (
        filters.shape[0] == LANES
        and q_feat.shape[0] % LANES == 0
        and peers % 8 == 0
        and lax.axis_size("tp") == 2
        and w_out.shape[1] % LANES == 0
    ):
        return fused_mixer(q_feat, k_feat, v_feat, stream, filters, w_out, peers)
    gated = gated_features(q_feat, k_feat, v_feat, filters)
    terms = jnp.dot(
        gated, lax.all_gather(w_out, "seq", axis=1, tiled=True), preferred_element_type=jnp.float32
    )
    accumulated_total = lax.psum_scatter(
        terms.astype(jnp.bfloat16), "tp", scatter_dimension=1, tiled=True
    ).astype(jnp.float32)
    return (stream.astype(jnp.float32) + accumulated_total).astype(jnp.bfloat16)


def solution(mesh):
    return jax.shard_map(
        local,
        mesh=mesh,
        in_specs=(
            P("seq", "tp"),
            P("seq", "tp"),
            P("seq", "tp"),
            P("seq", "tp"),
            P(("tp", "seq"), None),
            P("tp", "seq"),
        ),
        out_specs=P("seq", "tp"),
        check_vma=False,
    )
```

```python
import functools
import math

import jax
import jax.numpy as jnp
import numpy as np
from jax import lax
from jax.experimental import pallas as pl
from jax.experimental.pallas import tpu as pltpu
from jax.sharding import PartitionSpec as P

LANES = 128
GROUP = 16
PIECES = 4

def window_extent(total):
    chosen = 2
    for normalizing_multiplier in range(2, math.isqrt(total) + 1, 2):
        if total % normalizing_multiplier == 0:
            chosen = normalizing_multiplier
    return chosen


def make_tables(first, second, total):
    rows = jnp.arange(first, dtype=jnp.int32)
    half_rows = jnp.arange(first // 2, dtype=jnp.int32)
    columns = jnp.arange(second, dtype=jnp.int32)
    angle_one = (
        2.0 * math.pi / first * (rows[:, None] * half_rows[None, :] % first).astype(jnp.float32)
    )
    angle_two = (
        2.0 * math.pi / second * (columns[:, None] * columns[None, :] % second).astype(jnp.float32)
    )
    angle_twist = (
        2.0 * math.pi / total * (rows[:, None] * columns[None, :] % total).astype(jnp.float32)
    )
    return (
        jnp.cos(angle_one),
        jnp.sin(angle_one),
        jnp.cos(angle_two),
        jnp.sin(angle_two),
        jnp.cos(angle_twist),
        jnp.sin(angle_twist),
    )


def forward_transform(signal, tables, first, second):
    cosine_first, sin_one, cos_two, sin_two, cos_twist, sin_twist = tables
    chans = signal.shape[0]
    shaped = signal.reshape(chans, first // 2, second)
    highest = lax.Precision.HIGHEST
    real_a = jnp.einsum("kn,cnm->ckm", cosine_first, shaped, precision=highest)
    imaginary_left = -jnp.einsum("kn,cnm->ckm", sin_one, shaped, precision=highest)
    real_b = real_a * cos_twist + imaginary_left * sin_twist
    imag_b = imaginary_left * cos_twist - real_a * sin_twist
    real_x = jnp.einsum("ckn,nm->ckm", real_b, cos_two, precision=highest) + jnp.einsum(
        "ckn,nm->ckm", imag_b, sin_two, precision=highest
    )
    imag_x = jnp.einsum("ckn,nm->ckm", imag_b, cos_two, precision=highest) - jnp.einsum(
        "ckn,nm->ckm", real_b, sin_two, precision=highest
    )
    return (real_x, imag_x)


def inverse_transform(real_p, imag_p, tables, first, second):
    cosine_first, sin_one, cos_two, sin_two, cos_twist, sin_twist = tables
    highest = lax.Precision.HIGHEST
    real_d = jnp.einsum("ckn,nm->ckm", real_p, cos_two, precision=highest) - jnp.einsum(
        "ckn,nm->ckm", imag_p, sin_two, precision=highest
    )
    imag_d = jnp.einsum("ckn,nm->ckm", real_p, sin_two, precision=highest) + jnp.einsum(
        "ckn,nm->ckm", imag_p, cos_two, precision=highest
    )
    kernel_spectrum_real = real_d * cos_twist - imag_d * sin_twist
    imag_e = real_d * sin_twist + imag_d * cos_twist
    result = jnp.einsum(
        "kn,ckm->cnm", cosine_first, kernel_spectrum_real, precision=highest
    ) - jnp.einsum("kn,ckm->cnm", sin_one, imag_e, precision=highest)
    return result / (first * second)


def long_conv(mixed_cols, filters):
    chans, length = filters.shape
    total = 2 * length
    first = window_extent(total)
    second = total // first
    tables = make_tables(first, second, total)
    stacked = jnp.concatenate([mixed_cols.astype(jnp.float32), filters], axis=0)
    real_x, imag_x = forward_transform(stacked, tables, first, second)
    real_p = real_x[:chans] * real_x[chans:] - imag_x[:chans] * imag_x[chans:]
    imag_p = real_x[:chans] * imag_x[chans:] + imag_x[:chans] * real_x[chans:]
    result = inverse_transform(real_p, imag_p, tables, first, second)
    return result.reshape(chans, length)


def spectral_tables(length):
    total = 2 * length
    first = total // LANES
    slots = first // 2
    n_one = np.arange(slots)
    base = np.zeros((slots, 2, slots))
    for s in range(1, slots):
        angle = 2.0 * np.pi * (s * n_one % first) / first
        base[s, 0] = np.cos(angle)
        base[s, 1] = -np.sin(angle)
    base[0, 0] = 1.0
    base[0, 1] = 1.0 - 2.0 * (n_one % 2)
    outer = np.kron(base.reshape(first, slots), np.eye(GROUP))
    n_two = np.arange(LANES)
    k_two = np.arange(LANES)
    inner = np.zeros((slots, 2 * LANES, 2 * LANES))

    def wave(k_one, rows):
        turns = (first * rows[:, None] + k_one) * n_two[None, :] % total
        return np.exp(-2j * np.pi * turns / total)

    for s in range(1, slots):
        t = wave(s, k_two)
        inner[s] = np.block([[t.real, -t.imag], [t.imag, t.real]])
    half = LANES // 2
    zero = wave(0, k_two[:half])
    mid = wave(slots, k_two[:half])
    inner[0, :half, :LANES] = zero.real
    inner[0, half:LANES, LANES:] = mid.real
    inner[0, LANES : LANES + half, :LANES] = zero.imag
    inner[0, LANES + half :, LANES:] = mid.imag
    inner[0, LANES, :LANES] = 1.0 - 2.0 * (n_two % 2)
    cast = lambda a: np.ascontiguousarray(a).astype(jnp.bfloat16)
    return cast(outer), cast(outer.T), cast(inner), cast(inner.transpose(0, 2, 1))


def spectral_product(a, b, slot_zero):
    a_re, a_im = a[:LANES], a[LANES:]
    b_re, b_im = b[:LANES], b[LANES:]
    rr, ii = a_re * b_re, a_im * b_im
    p_re = rr - ii
    p_im = a_re * b_im + a_im * b_re
    if slot_zero:
        top = lax.broadcasted_iota(jnp.int32, p_re.shape, 0) == 0
        p_re = jnp.where(top, 0.5 * rr, p_re)
        p_im = jnp.where(top, 0.5 * ii, p_im)
    return jnp.concatenate([p_re, p_im], axis=0)


def mixer_kernel(
    peers,
    k_ref,
    v_ref,
    q_hbm,
    stream_hbm,
    taps_hbm,
    weights_hbm,
    outer_hbm,
    outer_t_hbm,
    inner_hbm,
    inner_t_hbm,
    out_ref,
    q_ref,
    stream_ref,
    taps_ref,
    outer_ref,
    outer_t_ref,
    inner_ref,
    inner_t_ref,
    sent,
    signal,
    result,
    returned,
    turned,
    spectrum,
    work,
    gated,
    weights,
    kept,
    shares,
    arrived,
    load_sem,
    send_one,
    recv_one,
    send_two,
    recv_two,
    send_weight,
    recv_weight,
    send_share,
    recv_share,
):
    me = lax.axis_index("seq")
    tp = lax.axis_index("tp")
    rows = k_ref.shape[0]
    slots = signal.shape[0]
    per = slots // peers
    total = 2 * slots * LANES
    mesh_ids = pl.DeviceIdType.MESH
    depth = peers // 4
    half = peers // 2
    width = weights.shape[2]
    layer, side, core = me // 4, (me // 2) % 2, me % 2

    loads = [
        pltpu.make_async_copy(source, target, load_sem.at[i])
        for i, (source, target) in enumerate(
            [
                (weights_hbm, weights.at[me]),
                (taps_hbm, taps_ref),
                (outer_hbm, outer_ref),
                (inner_hbm, inner_ref),
                (inner_t_hbm, inner_t_ref),
                (outer_t_hbm, outer_t_ref),
                (q_hbm, q_ref),
                (stream_hbm, stream_ref),
            ]
        )
    ]
    for load in loads:
        load.start()

    def block_at(zz, xx, cc):
        return (zz * 2 + xx) * 2 + cc

    piece = weights.shape[1] // PIECES

    def weight_copy(block, part, target, way):
        held = weights.at[block, pl.ds(part * piece, piece)]
        return pltpu.make_async_remote_copy(
            src_ref=held,
            dst_ref=held,
            send_sem=send_weight.at[block * PIECES + part, way],
            recv_sem=recv_weight.at[block * PIECES + part],
            device_id={"seq": target},
            device_id_type=mesh_ids,
        )

    to_core = block_at(layer, side, 1 - core)
    to_side = block_at(layer, 1 - side, core)

    def act(copy, sending):
        if sending:
            copy.start()
        else:
            copy.wait_send()

    def spread(block, part, sending, up, down):
        if up:

            @pl.when(layer + 1 < depth)
            def _():
                act(weight_copy(block, part, me + 4, 2), sending)

        if down:

            @pl.when(layer > 0)
            def _():
                act(weight_copy(block, part, me - 4, 3), sending)

        act(weight_copy(block, part, to_side, 1), sending)
        act(weight_copy(block, part, to_core, 0), sending)

    def arrive(block, part):
        weight_copy(block, part, to_core, 0).wait_recv()

    def at_distance(d, body):
        for sign in (-1, 1) if d else (1,):
            zz = layer + sign * d

            @pl.when((zz >= 0) & (zz < depth))
            def _():
                body(zz, sign)

    def from_layer(d, *parts):
        if d >= depth:
            return

        def body(zz, sign, part):
            block = block_at(zz, side, core)
            arrive(block, part)
            spread(block, part, True, sign < 0, sign > 0)

        for part in parts or range(PIECES):
            at_distance(d, functools.partial(body, part=part))

    def from_side(d, *parts):
        if d >= depth:
            return

        def body(zz, sign, part):
            block = block_at(zz, 1 - side, core)
            arrive(block, part)
            weight_copy(block, part, to_core, 0).start()

        for part in parts or range(PIECES):
            at_distance(d, functools.partial(body, part=part))

    def share_copy(b):
        return pltpu.make_async_remote_copy(
            src_ref=shares.at[b],
            dst_ref=arrived.at[b],
            send_sem=send_share.at[b],
            recv_sem=recv_share.at[b],
            device_id={"tp": 1 - tp},
            device_id_type=mesh_ids,
        )

    def project(d, turns=(0, 1)):
        def body(zz, sign, turn):
            xx = side if turn == 0 else 1 - side
            for part in range(PIECES):
                arrive(block_at(zz, xx, 1 - core), part)

            def step(i, carry):
                block = block_at(zz, xx, i)
                terms = jnp.dot(gated[...], weights[block], preferred_element_type=jnp.float32)
                b = block % half

                @pl.when(block // half == tp)
                def _():
                    kept[b] = terms

                @pl.when(block // half != tp)
                def _():
                    shares[b] = terms.astype(jnp.bfloat16)
                    share_copy(b).start()

                return carry

            lax.fori_loop(0, 2, step, 0)

        if d < depth:
            for turn in turns:
                at_distance(d, functools.partial(body, turn=turn))

    def finish(d):
        def body(zz, sign):
            @pl.when(zz * 4 // half == tp)
            def _():
                def step(i, carry):
                    b = (zz * 4 + i) % half
                    share_copy(b).wait_recv()
                    cols = pl.ds(pl.multiple_of(b * width, width), width)
                    added = kept[b] + arrived[b].astype(jnp.float32)
                    total = stream_ref[:, cols].astype(jnp.float32) + added
                    out_ref[:, cols] = total.astype(jnp.bfloat16)
                    return carry

                lax.fori_loop(0, 4, step, 0)

        if d < depth:
            at_distance(d, body)

    barrier = pltpu.get_barrier_semaphore()
    for i in range(1, peers):
        pl.semaphore_signal(
            barrier,
            inc=1,
            device_id={"seq": lax.rem(me + i, peers)},
            device_id_type=mesh_ids,
        )
    pl.semaphore_signal(barrier, inc=1, device_id={"tp": 1 - tp}, device_id_type=mesh_ids)

    def mix(p, carry):
        cols = pl.ds(pl.multiple_of(p * LANES, LANES), LANES)
        product = k_ref[:, cols].astype(jnp.float32) * v_ref[:, cols].astype(jnp.float32)
        sent[p] = product.astype(jnp.bfloat16).reshape(per, LANES, LANES)
        return carry

    loads[0].wait()
    pl.semaphore_wait(barrier, peers)
    for part in range(PIECES):
        spread(me, part, True, True, True)
    lax.fori_loop(0, peers, mix, 0)

    first_copies = []
    for i in range(1, peers):
        target = lax.rem(me + i, peers)
        copy = pltpu.make_async_remote_copy(
            src_ref=sent.at[target],
            dst_ref=signal.at[pl.ds(me * per, per)],
            send_sem=send_one.at[i],
            recv_sem=recv_one.at[i],
            device_id={"seq": target},
            device_id_type=mesh_ids,
        )
        copy.start()
        first_copies.append(copy)
    signal[pl.ds(me * per, per)] = sent[me]

    def outer_stage(source):
        def step(g, carry):
            lo = pl.ds(pl.multiple_of(g * 2 * GROUP, 2 * GROUP), GROUP)
            hi = pl.ds(pl.multiple_of(g * 2 * GROUP + GROUP, GROUP), GROUP)
            block = jnp.concatenate(
                [
                    source[:, lo, :].reshape(slots * GROUP, LANES),
                    source[:, hi, :].reshape(slots * GROUP, LANES),
                ],
                axis=1,
            )
            y = jnp.dot(outer_ref[...], block, preferred_element_type=jnp.float32)
            y = y.astype(jnp.bfloat16)
            work[:, :, lo, :] = y[:, :LANES].reshape(slots, 2, GROUP, LANES)
            work[:, :, hi, :] = y[:, LANES:].reshape(slots, 2, GROUP, LANES)
            return carry

        lax.fori_loop(0, LANES // (2 * GROUP), step, 0)

    def inner_forward(s):
        return jnp.dot(
            inner_ref[s],
            work[s].reshape(2 * LANES, LANES),
            preferred_element_type=jnp.float32,
        )

    def turn(n, carry):
        cols = pl.ds(pl.multiple_of(n * LANES, LANES), LANES)
        turned[n] = taps_ref[:, cols].T.astype(jnp.bfloat16)
        return carry

    loads[1].wait()
    lax.fori_loop(0, slots, turn, 0)
    loads[2].wait()
    outer_stage(turned)
    loads[3].wait()
    from_layer(1, 0)

    def tap_step(s, carry):
        spectrum[s] = inner_forward(s)
        return carry

    lax.fori_loop(0, slots, tap_step, 0, unroll=4)
    from_layer(1, 1)

    for copy in first_copies:
        copy.wait_recv()
    outer_stage(signal)
    from_layer(1, 2, 3)
    loads[4].wait()

    def middle(s, slot_zero):
        p = spectral_product(inner_forward(s), spectrum[s], slot_zero)
        q = jnp.dot(inner_t_ref[s], p.astype(jnp.bfloat16), preferred_element_type=jnp.float32)
        work[s] = q.astype(jnp.bfloat16).reshape(2, LANES, LANES)

    middle(0, True)

    def middle_step(s, carry):
        middle(s, False)
        return carry

    lax.fori_loop(1, slots // 2, middle_step, 0, unroll=4)
    from_layer(2, 0)
    lax.fori_loop(slots // 2, slots, middle_step, 0, unroll=4)
    from_layer(2, 1)

    loads[5].wait()

    def outer_back(g, carry):
        lo = pl.ds(pl.multiple_of(g * 2 * GROUP, 2 * GROUP), GROUP)
        hi = pl.ds(pl.multiple_of(g * 2 * GROUP + GROUP, GROUP), GROUP)
        block = jnp.concatenate(
            [
                work[:, :, lo, :].reshape(2 * slots * GROUP, LANES),
                work[:, :, hi, :].reshape(2 * slots * GROUP, LANES),
            ],
            axis=1,
        )
        y = jnp.dot(outer_t_ref[...], block, preferred_element_type=jnp.float32)
        y = (y * (2.0 / total)).astype(jnp.bfloat16)
        result[:, lo, :] = y[:, :LANES].reshape(slots, GROUP, LANES)
        result[:, hi, :] = y[:, LANES:].reshape(slots, GROUP, LANES)
        return carry

    lax.fori_loop(0, LANES // (2 * GROUP), outer_back, 0)

    second_copies = []
    for i in range(1, peers):
        target = lax.rem(me + i, peers)
        copy = pltpu.make_async_remote_copy(
            src_ref=result.at[pl.ds(target * per, per)],
            dst_ref=returned.at[me],
            send_sem=send_two.at[i],
            recv_sem=recv_two.at[i],
            device_id={"seq": target},
            device_id_type=mesh_ids,
        )
        copy.start()
        second_copies.append(copy)
    from_side(0)
    from_layer(2, 2, 3)
    from_side(1)
    from_layer(3)
    from_side(2)
    loads[6].wait()
    loads[7].wait()

    def gate(p, block):
        cols = pl.ds(pl.multiple_of(p * LANES, LANES), LANES)
        conv = block.reshape(rows, LANES).astype(jnp.float32)
        gated[:, cols] = (q_ref[:, cols].astype(jnp.float32) * conv).astype(jnp.bfloat16)

    gate(me, result[pl.ds(me * per, per)])
    for i, copy in enumerate(second_copies, 1):
        copy.wait_recv()
        source = lax.rem(me + peers - i, peers)
        gate(source, returned[source])
    project(0)
    project(1)
    finish(0)
    project(2)
    finish(1)
    project(3, (0,))
    from_side(3)
    project(3, (1,))
    finish(2)
    for d in range(4, depth):
        from_layer(d)
        from_side(d)
        project(d)
        finish(d - 1)
    if depth > 3:
        finish(depth - 1)

    for copy in first_copies + second_copies:
        copy.wait_send()
    for part in range(PIECES):
        spread(me, part, False, True, True)
    for d in range(depth):

        def settle(zz, sign):
            for part in range(PIECES):
                if d:
                    spread(block_at(zz, side, core), part, False, sign < 0, sign > 0)
                weight_copy(block_at(zz, 1 - side, core), part, to_core, 0).wait_send()

        at_distance(d, settle)

    def sent_share(b, carry):
        share_copy(b).wait_send()
        return carry

    lax.fori_loop(0, half, sent_share, 0)


def fused_mixer(q_feat, k_feat, v_feat, stream, filters, w_out, peers):
    rows, columns = q_feat.shape
    chans, length = filters.shape
    slots = length // LANES
    per = rows // LANES
    tables = spectral_tables(length)
    vmem = pl.BlockSpec(memory_space=pltpu.VMEM)
    anywhere = pl.BlockSpec(memory_space=pl.ANY)
    bf16 = jnp.bfloat16
    depth, width = w_out.shape
    half = peers // 2
    dma = pltpu.SemaphoreType.DMA
    return pl.pallas_call(
        functools.partial(mixer_kernel, peers),
        out_shape=jax.ShapeDtypeStruct((rows, columns), bf16),
        in_specs=[vmem] * 2 + [anywhere] * 8,
        out_specs=vmem,
        scratch_shapes=[
            pltpu.VMEM((rows, columns), bf16),
            pltpu.VMEM((rows, columns), bf16),
            pltpu.VMEM((chans, length), jnp.float32),
        ]
        + [pltpu.VMEM(t.shape, bf16) for t in tables]
        + [
            pltpu.VMEM((peers, per, LANES, LANES), bf16),
            pltpu.VMEM((slots, LANES, LANES), bf16),
            pltpu.VMEM((slots, LANES, LANES), bf16),
            pltpu.VMEM((peers, per, LANES, LANES), bf16),
            pltpu.VMEM((slots, LANES, LANES), bf16),
            pltpu.VMEM((slots, 2 * LANES, LANES), jnp.float32),
            pltpu.VMEM((slots, 2, LANES, LANES), bf16),
            pltpu.VMEM((rows, columns), bf16),
            pltpu.VMEM((peers, depth, width), bf16),
            pltpu.VMEM((half, rows, width), jnp.float32),
            pltpu.VMEM((half, rows, width), bf16),
            pltpu.VMEM((half, rows, width), bf16),
            dma((8,)),
            dma((peers,)),
            dma((peers,)),
            dma((peers,)),
            dma((peers,)),
            dma((peers * PIECES, 4)),
            dma((peers * PIECES,)),
            dma((half,)),
            dma((half,)),
        ],
        compiler_params=pltpu.CompilerParams(
            collective_id=0, has_side_effects=True, vmem_limit_bytes=58 * 1024 * 1024
        ),
        cost_estimate=pl.CostEstimate(
            flops=2 * rows * depth * width * peers,
            bytes_accessed=16 * 1024 * 1024,
            transcendentals=0,
        ),
    )(k_feat, v_feat, q_feat, stream, filters, w_out, *[jnp.asarray(t) for t in tables])


def gated_features(q_feat, k_feat, v_feat, filters):
    mixed = (k_feat.astype(jnp.float32) * v_feat.astype(jnp.float32)).astype(jnp.bfloat16)
    sent_mixed = lax.all_to_all(mixed.T, "seq", split_axis=0, concat_axis=1, tiled=True)
    conv_out = long_conv(sent_mixed, filters).astype(jnp.bfloat16)
    returned_output = lax.all_to_all(conv_out, "seq", split_axis=1, concat_axis=0, tiled=True)
    return (q_feat.astype(jnp.float32) * returned_output.T.astype(jnp.float32)).astype(
        jnp.bfloat16
    )


def local(q_feat, k_feat, v_feat, stream, filters, w_out):
    peers = lax.axis_size("seq")
    if (
        filters.shape[0] == LANES
        and q_feat.shape[0] % LANES == 0
        and peers % 8 == 0
        and lax.axis_size("tp") == 2
        and w_out.shape[1] % LANES == 0
    ):
        return fused_mixer(q_feat, k_feat, v_feat, stream, filters, w_out, peers)
    gated = gated_features(q_feat, k_feat, v_feat, filters)
    terms = jnp.dot(
        gated, lax.all_gather(w_out, "seq", axis=1, tiled=True), preferred_element_type=jnp.float32
    )
    accumulated_total = lax.psum_scatter(
        terms.astype(jnp.bfloat16), "tp", scatter_dimension=1, tiled=True
    ).astype(jnp.float32)
    return (stream.astype(jnp.float32) + accumulated_total).astype(jnp.bfloat16)


def solution(mesh):
    return jax.shard_map(
        local,
        mesh=mesh,
        in_specs=(
            P("seq", "tp"),
            P("seq", "tp"),
            P("seq", "tp"),
            P("seq", "tp"),
            P(("tp", "seq"), None),
            P("tp", "seq"),
        ),
        out_specs=P("seq", "tp"),
        check_vma=False,
    )
```
